512 devices in a mesh: region: 16 (over y, core), dev: 32 (over z, x).
Axes of the slice: x: 4, y: 8, z: 8, core: 2. Of those that a mesh axis runs over, the one named last changes fastest.
Arguments:
- data_panel: bfloat16 [64, 262144], P(None, ('region', 'dev'))
- reg_panel: bfloat16 [64, 524288], P(None, ('region', 'dev'))
- prev_panel: float32 [64, 524288], P(None, ('region', 'dev'))
- lower_block: float32 [64, 64], replicated
- sens_tiles: bfloat16 [4096, 8, 128, 128], P(('region', 'dev')), may hold values from -0.1875 to 0.1875
- sens_src: int32 [4096, 8], P(('region', 'dev')), may hold values from 0 to 31, as said below
- touched: int32 [16384], P(('region', 'dev')), may hold values from 0 to 3
- couple_tiles: bfloat16 [4096, 2, 128, 128], P(('region', 'dev')), may hold values from -0.375 to 0.375
- couple_map: int32 [4096, 2], P(('region', 'dev')), may hold values from 0 to 7
- grad_tiles: bfloat16 [4096, 3, 128, 128], P(('region', 'dev')), may hold values from -0.3125 to 0.3125
- grad_map: int32 [4096, 3], P(('region', 'dev')), may hold values from 0 to 9, as said below
Outputs:
- panel_q: float32 [64, 524288], P(None, ('region', 'dev'))
- factor: float32 [64, 64], replicated
The draws below stay inside these ranges and needn't reach their ends.
Inputs may be any that keep to these rules, and one draw needn't show every extreme that they name: `sens_src`: on each device's 8 cell blocks every device index of the region appears at least once. `couple_map`: values below 4 name blocks of the region before, the others blocks of the region after. `grad_map`: the first column of local block i is i + 1 (the block itself), the others lie in i to i + 2; local block 0 reads value 0 and local block 7 reads value 8 + 1.
All inputs are finite; a program needn't handle non-finite values.
Results may differ from the reference program's by a relative error of at most 0.0029.
Values may be sent and summed in bfloat16 or wider, within the bound.
A program may use at most 64 MiB of HBM per device.

```python
import math
import jax
import jax.numpy as jnp
from jax import lax

PANEL = 64
BLK = 128
NB_DEV = 8
DB_DEV = 4
K = 8
KC = 2
KG = 3
PEERS = 32
REGIONS = 16
CELLBLOCKS = 4096
MODEL_CELL_COUNT = 524288
SENSOR_READ_COUNT = 262144
PAIRS = 16384
DEVICES = 512


def shared_signs(key):
    return jax.random.rademacher(key, (PANEL, 1), dtype=jnp.float32)


def dependent_panel(key, random_signs, common_part, own_share, panel_columns):
    key_gain, key_scale = jax.random.split(key, 2)
    gains = jax.random.uniform(key_gain, (PANEL, 1), jnp.float32, 0.7, 1.3)
    column_scale = jnp.exp(jax.random.uniform(key_scale, (1, panel_columns), jnp.float32, math.log(0.5), math.log(2.0)))
    return 3.0 * random_signs * gains * common_part * column_scale + 0.05 * own_share


def draw_data_panel(key, part):
    random_signs = shared_signs(key)
    key = jax.random.fold_in(key, 61)
    key_common, key_own, remaining_key = jax.random.split(key, 3)
    common_part = jax.random.truncated_normal(key_common, -3.0, 3.0, (1, SENSOR_READ_COUNT), jnp.float32)
    own_share = jax.random.truncated_normal(key_own, -3.0, 3.0, (PANEL, SENSOR_READ_COUNT), jnp.float32)
    return dependent_panel(remaining_key, random_signs, common_part, own_share, SENSOR_READ_COUNT).astype(jnp.bfloat16)


def draw_reg_panel(key, part):
    random_signs = shared_signs(key)
    key = jax.random.fold_in(key, 67)
    key_common, key_own, remaining_key = jax.random.split(key, 3)
    common_part = jax.random.truncated_normal(key_common, -3.0, 3.0, (1, MODEL_CELL_COUNT), jnp.float32)
    own_share = jax.random.truncated_normal(key_own, -3.0, 3.0, (PANEL, MODEL_CELL_COUNT), jnp.float32)
    return dependent_panel(remaining_key, random_signs, common_part, own_share, MODEL_CELL_COUNT).astype(jnp.bfloat16)


def draw_sens_src(key, part):
    key = jax.random.fold_in(key, 11)
    tile_count = NB_DEV * K
    device_keys = jax.random.split(key, DEVICES)

    def draw_device(device_key):
        key_first, key_extra, key_order = jax.random.split(device_key, 3)
        covering = jax.random.permutation(key_first, PEERS).astype(jnp.int32)
        extra_slots = jax.random.randint(key_extra, (tile_count - PEERS,), 0, PEERS).astype(jnp.int32)
        joined = jnp.concatenate([covering, extra_slots])
        return jax.random.permutation(key_order, joined)
    return jax.vmap(draw_device)(device_keys).reshape(CELLBLOCKS, K).astype(jnp.int32)


def draw_grad_map(key, part):
    key = jax.random.fold_in(key, 23)
    local_block = jnp.arange(CELLBLOCKS, dtype=jnp.int32) % NB_DEV
    offsets = jax.random.randint(key, (CELLBLOCKS, KG - 1), 0, 3).astype(jnp.int32)
    nearby = local_block[:, None] + offsets
    first_col = jnp.where(local_block == 0, 0, nearby[:, 0])
    last_col = jnp.where(local_block == NB_DEV - 1, NB_DEV + 1, nearby[:, KG - 2])
    nearby = nearby.at[:, 0].set(first_col).at[:, KG - 2].set(last_col)
    return jnp.concatenate([(local_block + 1)[:, None], nearby], axis=1).astype(jnp.int32)


def draw_prev_panel(key, part):
    key = jax.random.fold_in(key, 37)
    key_rows, key_cells, key_base = jax.random.split(key, 3)
    row_scale = jnp.exp(jax.random.uniform(key_rows, (PANEL, 1), jnp.float32, math.log(0.3), math.log(3.0)))
    ramp = 1.0 + 2.0 * jnp.arange(MODEL_CELL_COUNT, dtype=jnp.float32) / max(MODEL_CELL_COUNT - 1, 1)
    cell_scale = jnp.exp(jax.random.uniform(key_cells, (1, MODEL_CELL_COUNT), jnp.float32, math.log(0.3), math.log(3.0))) * ramp[None, :]
    base_draw = jax.random.normal(key_base, (PANEL, MODEL_CELL_COUNT), jnp.float32)
    return (base_draw * row_scale * cell_scale).astype(jnp.float32)


def draw_lower_block(key, part):
    key = jax.random.fold_in(key, 53)
    noise = jax.random.normal(key, (PANEL, PANEL), jnp.float32)
    return (0.003 * noise).astype(jnp.float32)


def set_ends(drawn, rng, smallest, largest):
    spot = [jax.random.randint(jax.random.fold_in(rng, axis), (), 0, length) for axis, length in enumerate(drawn.shape)]
    widest = drawn.shape.index(max(drawn.shape))
    next_to = spot[:widest] + [(spot[widest] + 1) % drawn.shape[widest]] + spot[widest + 1:]
    return drawn.at[tuple(spot)].set(smallest).at[tuple(next_to)].set(largest)


def level_of(key, shape, cuts, low, top_value):
    def one(dim, parts):
        steps = jax.random.uniform(jax.random.fold_in(jax.random.fold_in(key, 6), dim), (parts,), jnp.float32, low / len(cuts), top_value / len(cuts))
        return jnp.repeat(jnp.exp(steps), shape[dim] // parts).reshape((-1,) + (1,) * (len(shape) - dim - 1))

    level = one(*cuts[0])
    for cut in cuts[1:]:
        level = level * one(*cut)
    return level


def normal_values(stream_key, shape, width, most, cuts=(), held_as=jnp.bfloat16):
    drawn = jax.random.normal(stream_key, shape, jnp.float32) * width
    if len(cuts) > 0:
        drawn = level_of(stream_key, shape, cuts, -0.22, 0.18) * drawn
    return jnp.clip(drawn, min=-most, max=most).astype(held_as)


def setup_inputs(seed: int = 0) -> dict:
    splits = jax.random.split(jax.random.key(seed), 12)
    return {
        "data_panel": draw_data_panel(jax.random.fold_in(splits[11], 71), 0),
        "reg_panel": draw_reg_panel(jax.random.fold_in(splits[11], 71), 0),
        "prev_panel": draw_prev_panel(jax.random.fold_in(splits[11], 71), 0),
        "lower_block": draw_lower_block(jax.random.fold_in(splits[11], 71), 0),
        "sens_tiles": normal_values(splits[4], (CELLBLOCKS, K, BLK, BLK), (K * BLK) ** -0.5, 0.1875, ((0, 512),)),
        "sens_src": draw_sens_src(jax.random.fold_in(splits[11], 71), 0),
        "touched": set_ends(jax.random.randint(splits[6], (PAIRS,), 0, DB_DEV), jax.random.fold_in(splits[6], 1), 0, DB_DEV - 1).astype(jnp.int32),
        "couple_tiles": normal_values(splits[7], (CELLBLOCKS, KC, BLK, BLK), (KC * BLK) ** -0.5, 0.375, ((0, 512),)),
        "couple_map": set_ends(jax.random.randint(splits[8], (CELLBLOCKS, KC), 0, 2 * DB_DEV), jax.random.fold_in(splits[8], 1), 0, (2 * DB_DEV) - 1).astype(jnp.int32),
        "grad_tiles": normal_values(splits[9], (CELLBLOCKS, KG, BLK, BLK), (KG * BLK) ** -0.5, 0.3125, ((0, 512),)),
        "grad_map": draw_grad_map(jax.random.fold_in(splits[11], 71), 0),
    }


penalty_weight = 0.5

def tile_sum(picked, tiles):
    return jnp.einsum('pbkr,bkrc->bpc', picked.astype(jnp.float32), tiles.astype(jnp.float32))

def cholesky_pass(matrix):
    gram_sum = jnp.dot(matrix, matrix.T, precision=lax.Precision.HIGHEST) / MODEL_CELL_COUNT
    lower_factor = jnp.linalg.cholesky(gram_sum)
    identity = jnp.eye(gram_sum.shape[0], dtype=gram_sum.dtype)
    inverse = lax.linalg.triangular_solve(lower_factor, identity, left_side=True, lower=True)
    return (jnp.dot(inverse, matrix, precision=lax.Precision.HIGHEST), lower_factor)

def reference(data_panel, reg_panel, prev_panel, lower_block, sens_tiles, sens_src, touched, couple_tiles, couple_map, grad_tiles, grad_map):
    data_blocks = data_panel.reshape(PANEL, DEVICES, DB_DEV, BLK)
    reg_blocks = reg_panel.reshape(PANEL, DEVICES, NB_DEV, BLK)
    zero_side = jnp.zeros((PANEL, DB_DEV, BLK), data_panel.dtype)
    zero_rim = jnp.zeros((PANEL, 1, BLK), reg_panel.dtype)

    def per_device(device):
        region = device // PEERS
        first_block = device * NB_DEV
        sources = lax.dynamic_slice_in_dim(sens_src, first_block, NB_DEV, 0)
        wanted = lax.dynamic_slice_in_dim(touched, device * PEERS, PEERS, 0)
        chosen = wanted[sources]
        owner_device = region * PEERS + sources
        direct = tile_sum(data_blocks[:, owner_device, chosen], lax.dynamic_slice_in_dim(sens_tiles, first_block, NB_DEV, 0))
        lower_side = jnp.where(region > 0, data_blocks[:, jnp.maximum(device - PEERS, 0)], zero_side)
        upper_side = jnp.where(region < REGIONS - 1, data_blocks[:, jnp.minimum(device + PEERS, DEVICES - 1)], zero_side)
        both_sides = jnp.concatenate([lower_side, upper_side], axis=1)
        couple_rows = lax.dynamic_slice_in_dim(couple_map, first_block, NB_DEV, 0)
        coupled = tile_sum(both_sides[:, couple_rows], lax.dynamic_slice_in_dim(couple_tiles, first_block, NB_DEV, 0))
        behind = jnp.where(device > 0, reg_blocks[:, jnp.maximum(device - 1, 0), NB_DEV - 1:], zero_rim)
        following = jnp.where(device < DEVICES - 1, reg_blocks[:, jnp.minimum(device + 1, DEVICES - 1), :1], zero_rim)
        extended = jnp.concatenate([behind, reg_blocks[:, device], following], axis=1)
        grad_rows = lax.dynamic_slice_in_dim(grad_map, first_block, NB_DEV, 0)
        gradient = tile_sum(extended[:, grad_rows], lax.dynamic_slice_in_dim(grad_tiles, first_block, NB_DEV, 0))
        return direct + coupled + penalty_weight * gradient
    pieces = lax.map(per_device, jnp.arange(DEVICES, dtype=jnp.int32))
    combined = jnp.transpose(pieces, (2, 0, 1, 3)).reshape(PANEL, MODEL_CELL_COUNT)
    adjoint = combined - jnp.dot(lower_block, prev_panel, precision=lax.Precision.HIGHEST)
    first_q, first_lower = cholesky_pass(adjoint)
    panel_q, second_lower = cholesky_pass(first_q)
    factor = jnp.transpose(jnp.dot(first_lower, second_lower, precision=lax.Precision.HIGHEST))
    return (panel_q, factor)
```

```python
import functools

import jax
import jax.numpy as jnp
from jax import lax
from jax.experimental import pallas as pl
from jax.experimental.pallas import tpu as pltpu
from jax.sharding import PartitionSpec as P

F32 = jnp.float32
BF16 = jnp.bfloat16
SLICES = 4
BLK = 128
X_CHIPS = 4


def two_sum(a, b):
    s = a + b
    t = s - a
    return s, (a - (s - t)) + (b - t)


def cut(value, sigma):
    top = (value + sigma) - sigma
    return top, value - top


def eliminate(aug, rows):
    blocks = [aug[8 * b : 8 * b + 8, :] for b in range(rows // 8)]
    sub = lax.broadcasted_iota(jnp.int32, (8, 128), 0)
    out = []
    for b in range(rows // 8):
        live = len(blocks)
        cols = [
            [jnp.broadcast_to(blk[:, 8 * b + k : 8 * b + k + 1], (8, 128)) for blk in blocks]
            for k in range(8)
        ]
        head = blocks[0]
        pivots = jnp.ones((8, 128), F32)
        for k in range(8):
            pivot = jnp.broadcast_to(cols[k][0][k : k + 1, :], (8, 128))
            inv = 1.0 / pivot
            pivots = jnp.where(sub == k, pivot, pivots)
            factor = [c * inv for c in cols[k]]
            factor[0] = jnp.where(sub > k, factor[0], 0.0)
            for m in range(k + 1, 8):
                across = jnp.broadcast_to(cols[m][0][k : k + 1, :], (8, 128))
                cols[m] = [c - f * across for c, f in zip(cols[m], factor)]
            row = jnp.broadcast_to(head[k : k + 1, :], (8, 128))
            head = head - factor[0] * row
            blocks = [head] + [blk - f * row for blk, f in zip(blocks[1:], factor[1:])]
        root = lax.rsqrt(pivots)
        root = root * (1.5 - (0.5 * pivots) * (root * root))
        out.append(head * root)
        blocks = blocks[1:]
    return jnp.concatenate(out, axis=0)


def split3(v):
    hi = v.astype(BF16)
    r = v - hi.astype(F32)
    mid = r.astype(BF16)
    return hi, mid, (r - mid.astype(F32)).astype(BF16)


def finish_kernel(g_ref, s_ref, q_ref, f_ref):
    n = 64
    g = g_ref[...]
    lane = lax.broadcasted_iota(jnp.int32, (n, 128), 1)
    subl = lax.broadcasted_iota(jnp.int32, (n, 128), 0)
    left = lane < n
    eye_right = (lane == subl + n).astype(F32)
    eye = (lane == subl).astype(F32)
    low_part = jnp.where(left, pltpu.roll(g, n, 1), 0.0)
    hi_part = jnp.where(left, g, 0.0)
    first = eliminate(hi_part + eye_right, n)

    w = jnp.where(left, pltpu.roll(first, n, 1), 0.0)
    wsig = jnp.max(jnp.abs(w), axis=1, keepdims=True) * 131072.0
    gsig = jnp.max(jnp.abs(hi_part), axis=0, keepdims=True) * 131072.0
    ws = []
    r = w
    for i in range(4):
        top, r = cut(r, wsig * (2.0 ** (-7 * i)))
        ws.append(top.astype(BF16)[:, :n])
    gs = []
    r = hi_part
    for i in range(3):
        top, r = cut(r, gsig * (2.0 ** (-7 * i)))
        gs.append(top.astype(BF16))
    r = r + low_part
    for i in range(3, 6):
        top, r = cut(r, gsig * (2.0 ** (-7 * i)))
        gs.append(top.astype(BF16))
    hi = lo = None
    for level in range(6):
        pairs = [(i, level - i) for i in range(4) if 0 <= level - i < 6]
        lhs = jnp.concatenate([ws[i] for i, _ in pairs], axis=1)
        rhs = jnp.concatenate([gs[j] for _, j in pairs], axis=0)
        term = jnp.dot(lhs, rhs, preferred_element_type=F32)
        if hi is None:
            hi, lo = term, jnp.zeros_like(term)
        else:
            hi, e = two_sum(hi, term)
            lo = lo + e
    t = hi + lo
    g2 = lax.dot_general(
        t, w, (((1,), (1,)), ((), ())), precision=lax.Precision.HIGHEST, preferred_element_type=F32
    )
    zero = jnp.zeros((n, n), F32)
    second = eliminate(jnp.concatenate([g2, zero], axis=1) + eye_right, n)
    w2 = jnp.where(left, pltpu.roll(second, n, 1), 0.0)
    both = jnp.dot(second[:, :n], first[:, :n], precision=lax.Precision.HIGHEST, preferred_element_type=F32)
    f_ref[...] = both
    m = jnp.dot(w2[:, :n], w[:, :n], precision=lax.Precision.HIGHEST, preferred_element_type=F32)
    parts = jnp.concatenate([jnp.concatenate([p] * SLICES, axis=1) for p in split3(m)], axis=0)
    for c in range(4):
        res = jnp.dot(parts, s_ref[:, 256 * c : 256 * c + 256], preferred_element_type=F32)
        q_ref[:, 256 * c : 256 * c + 256] = res[:n] + (res[n : 2 * n] + res[2 * n :])


def finish(g, s):
    vm = pl.BlockSpec(memory_space=pltpu.VMEM)
    return pl.pallas_call(
        finish_kernel,
        out_shape=(jax.ShapeDtypeStruct((64, 1024), F32), jax.ShapeDtypeStruct((64, 64), F32)),
        in_specs=[vm, vm],
        out_specs=(vm, vm),
        compiler_params=pltpu.CompilerParams(vmem_limit_bytes=32 * 2**20),
        name="finish",
    )(g, s)


def gram_local(a):
    n = 64
    sig = jnp.max(jnp.abs(a), axis=1, keepdims=True) * 131072.0
    parts = []
    r = a
    for i in range(SLICES):
        top, r = cut(r, sig * (2.0 ** (-7 * i)))
        parts.append(top.astype(BF16))
    s = jnp.concatenate(parts, axis=0)
    p = lax.dot_general(s, s, (((1,), (1,)), ((), ())), preferred_element_type=F32)
    order = [(0, 0), (1, 0), (0, 1), (2, 0), (1, 1), (3, 0), (2, 1), (3, 1)]
    hi = lo = None
    for i, h in order:
        term = p[n * i : n * i + n, 128 * h : 128 * h + 128]
        if hi is None:
            hi, lo = term, jnp.zeros_like(term)
        else:
            hi, e = two_sum(hi, term)
            lo = lo + e
    hi, e = two_sum(hi, pltpu.roll(hi, n, 1))
    lo = (lo + pltpu.roll(lo, n, 1)) + e
    hi, lo = hi + lo, lo - ((hi + lo) - hi)
    lane = lax.broadcasted_iota(jnp.int32, (n, 128), 1)
    return s, jnp.where(lane < n, hi, pltpu.roll(lo, n, 1))


MESH = pl.DeviceIdType.MESH


def gather_kernel(
    sizes,
    data, reg, prev, low, touched_any, touched, sens, src, couple, cmap, grad, gmap,
    s_out, g_out,
    zbs, compact, xs, nb, ext, prev_v, sens_v, couple_v, grad_v, asked, adj, s_v, gpart, rs, zs, ys, ag,
    l_sem, z_send, z_recv, x_send, x_recv, n_send, n_recv, t_send, t_recv, a_send, a_recv,
):
    xn, zn, rn, nbl, dbl, kk, kc, kg = sizes
    n = 64
    yn, gn = rn // 2, 2 * xn
    dn = xn * zn
    rows = n // gn
    half = zn // 2
    r = lax.axis_index("region")
    d = lax.axis_index("dev")
    y, core = r // 2, r % 2
    z, x = d // xn, d % xn
    piece = x * 2 + core

    mine = zbs[0]
    below = [mine] + list(zbs[1:half])
    above = [mine] + list(zbs[half : 2 * half - 1])
    across = zbs[2 * half - 1]

    local = []

    def fetch(source, target):
        c = pltpu.make_async_copy(source, target, l_sem.at[len(local)])
        c.start()
        local.append(c)
        return c

    own = [fetch(data.at[:, pl.ds(BLK * b, BLK)], mine.at[b]) for b in range(dbl)]
    rim = [fetch(reg.at[:, pl.ds(BLK * b, BLK)], ext.at[b + 1]) for b in range(nbl)]
    prev_c = fetch(prev, prev_v)
    grad_c = fetch(grad, grad_v)
    couple_c = fetch(couple, couple_v)
    sens_c = fetch(sens, sens_v)

    def group(o):
        q = (piece + o) % gn
        return (y * 2 + q % 2, z * xn + q // 2)

    def along_z(o):
        return (r, ((z + o) % zn) * xn + x)

    def along_y(o):
        return (((y + o) % yn) * 2 + core, d)

    def along_x(o):
        return (r, z * xn + (x + o) % xn)

    up, down = ((r + 1) % rn, d), ((r + rn - 1) % rn, d)
    g = r * dn + d
    g_up, g_down = (g + 1) % (rn * dn), (g + rn * dn - 1) % (rn * dn)
    after, before = (g_up // dn, g_up % dn), (g_down // dn, g_down % dn)
    reached = [group(o) for o in range(1, gn)] + [along_z(o) for o in range(1, zn)]
    reached += [along_y(o) for o in range(1, yn)] + [up, down, after, before]
    barrier = pltpu.get_barrier_semaphore()
    for who in reached:
        pl.semaphore_signal(barrier, inc=1, device_id=who, device_id_type=MESH)
    pl.semaphore_wait(barrier, len(reached))

    def remote(source, target, send, recv, who):
        c = pltpu.make_async_remote_copy(
            src_ref=source, dst_ref=target, send_sem=send, recv_sem=recv,
            device_id=who, device_id_type=MESH,
        )
        c.start()
        return c

    sent = []
    asks = []
    for o in range(1, xn):
        asks.append(remote(touched_any, asked.at[xn - o - 1], t_send.at[o - 1], t_recv.at[o - 1], along_x(o)))
    sent += asks
    for c in own:
        c.wait()

    def ring(step):
        mid = dbl // 2
        if step < half - 1:
            pairs = [(below[step], below[step + 1]), (above[step], above[step + 1])]
        else:
            low_half, high_half = pl.ds(0, mid), pl.ds(mid, dbl - mid)
            pairs = [(below[step].at[low_half], across.at[low_half]), (above[step].at[high_half], across.at[high_half])]
        return [
            remote(source, target, z_send.at[way, step], z_recv.at[way, step], along_z(1 if way == 0 else zn - 1))
            for way, (source, target) in enumerate(pairs)
        ]

    x_copies = []

    def hand_on(slot, zz, held):
        for o in range(1, xn):
            xs[o - 1, slot] = held[asked[o - 1, 0, zz * xn + x]]
            x_copies.append(
                remote(xs.at[o - 1, slot], compact.at[zz * xn + x],
                       x_send.at[o - 1, slot], x_recv.at[o - 1, slot], along_x(o))
            )
        compact[zz * xn + x] = held[touched[zz * xn + x]]

    moves = ring(0)
    sent += moves
    for c in rim:
        c.wait()
    near = [
        remote(mine, nb.at[pl.ds(0, dbl)], n_send.at[0], n_recv.at[0], up),
        remote(mine, nb.at[pl.ds(dbl, dbl)], n_send.at[1], n_recv.at[1], down),
        remote(ext.at[nbl], ext.at[0], n_send.at[2], n_recv.at[2], after),
        remote(ext.at[1], ext.at[nbl + 1], n_send.at[3], n_recv.at[3], before),
    ]
    sent += near
    for c in asks:
        c.wait_recv()
    hand_on(0, z, mine)

    prev_c.wait()
    adj[...] = -jnp.dot(low[...], prev_v[...], precision=lax.Precision.HIGHEST, preferred_element_type=F32)

    def gradient(first, last):
        for b in range(first, last):
            lhs = jnp.concatenate([ext[gmap[b, j]] for j in range(kg)], axis=1)
            part = jnp.dot(lhs, grad_v[b].reshape(kg * BLK, BLK), preferred_element_type=F32)
            adj[:, BLK * b : BLK * b + BLK] += 0.5 * part

    def coupling(first, last):
        for b in range(first, last):
            lhs = jnp.concatenate([nb[cmap[b, j]] for j in range(kc)], axis=1)
            part = jnp.dot(lhs, couple_v[b].reshape(kc * BLK, BLK), preferred_element_type=F32)
            adj[:, BLK * b : BLK * b + BLK] += part

    for step in range(half):
        for c in moves:
            c.wait_recv()
        if step < half - 1:
            moves = ring(step + 1)
            sent += moves
            hand_on(2 * step + 1, (z + zn - step - 1) % zn, below[step + 1])
            hand_on(2 * step + 2, (z + step + 1) % zn, above[step + 1])
        else:
            hand_on(zn - 1, (z + half) % zn, across)
        if step == 0:
            grad_c.wait()
            couple_c.wait()
            for c in near:
                c.wait_recv()

            @pl.when(g == 0)
            def _():
                ext[0] = jnp.zeros((n, BLK), BF16)

            @pl.when(g == rn * dn - 1)
            def _():
                ext[nbl + 1] = jnp.zeros((n, BLK), BF16)

            @pl.when(r == 0)
            def _():
                nb[pl.ds(0, dbl)] = jnp.zeros((dbl, n, BLK), BF16)

            @pl.when(r == rn - 1)
            def _():
                nb[pl.ds(dbl, dbl)] = jnp.zeros((dbl, n, BLK), BF16)

            gradient(0, nbl)
            coupling(0, nbl)
    sens_c.wait()
    for c in x_copies:
        c.wait_recv()
    for b in range(nbl):
        lhs = jnp.concatenate([compact[src[b, k]] for k in range(kk)], axis=1)
        part = jnp.dot(lhs, sens_v[b].reshape(kk * BLK, BLK), preferred_element_type=F32)
        adj[:, BLK * b : BLK * b + BLK] += part

    s, gram = gram_local(adj[...])
    s_v[...] = s
    s_copy = fetch(s_v, s_out)
    gram = gram * (1.0 / (rn * dn * nbl * BLK))
    for q in range(gn):
        gpart[q] = gram[rows * q : rows * q + rows, :]

    lane = lax.broadcasted_iota(jnp.int32, (rows, BLK), 1)

    def total(ref, count):
        hi = ref[0]
        lo = jnp.zeros_like(hi)
        for q in range(1, count):
            hi, e = two_sum(hi, ref[q])
            lo = lo + e
        lo = jnp.where(lane < n, lo, hi)
        hi_part = hi
        low_sum = pltpu.roll(lo, n, 1)
        tail = jnp.where(lane < n, low_sum, 0.0) + jnp.where(lane < n, lo, 0.0)
        top = jnp.where(lane < n, hi_part, 0.0)
        big = top + tail
        rest = tail - (big - top)
        return jnp.where(lane < n, big, pltpu.roll(rest, n, 1))

    def exchange(stage, count, mine, box, who, source):
        copies = []
        for o in range(1, count):
            copies.append(
                remote(source(o), box.at[mine], a_send.at[stage, o - 1], a_recv.at[stage, o - 1], who(o))
            )
        return copies

    copies = exchange(0, gn, piece, rs, group, lambda o: gpart.at[(piece + o) % gn])
    rs[piece] = gpart[piece]
    for c in copies:
        c.wait_recv()
    sent += copies
    zs[z] = total(rs, gn)
    copies = exchange(1, zn, z, zs, along_z, lambda o: zs.at[z])
    for c in copies:
        c.wait_recv()
    sent += copies
    ys[y] = total(zs, zn)
    copies = exchange(2, yn, y, ys, along_y, lambda o: ys.at[y])
    for c in copies:
        c.wait_recv()
    sent += copies
    ag[piece] = total(ys, yn)
    copies = exchange(3, gn, piece, ag, group, lambda o: ag.at[piece])
    for c in copies:
        c.wait_recv()
    sent += copies
    for q in range(gn):
        g_out[rows * q : rows * q + rows, :] = ag[q]
    for c in sent + x_copies:
        c.wait_send()
    s_copy.wait()


def gather(xn, data, reg, prev, low, sens, src, touched, couple, cmap, grad, gmap):
    zn = lax.axis_size("dev") // xn
    rn = lax.axis_size("region")
    n = data.shape[0]
    nbl, kk = sens.shape[0], sens.shape[1]
    kc, kg = couple.shape[1], grad.shape[1]
    dbl = data.shape[1] // BLK
    gn, yn, dn = 2 * xn, rn // 2, xn * zn
    rows = n // gn
    most = max(gn, zn, yn) - 1
    vm = pl.BlockSpec(memory_space=pltpu.VMEM)
    sm = pl.BlockSpec(memory_space=pltpu.SMEM)
    hbm = pl.BlockSpec(memory_space=pl.ANY)
    sem = pltpu.SemaphoreType.DMA
    width = nbl * BLK
    sizes = (xn, zn, rn, nbl, dbl, kk, kc, kg)
    row = touched.reshape(1, dn)
    return pl.pallas_call(
        functools.partial(gather_kernel, sizes),
        out_shape=(
            jax.ShapeDtypeStruct((SLICES * n, width), BF16),
            jax.ShapeDtypeStruct((n, BLK), F32),
        ),
        in_specs=[hbm, hbm, hbm, vm, hbm, sm, hbm, sm, hbm, sm, hbm, sm],
        out_specs=(hbm, vm),
        scratch_shapes=[
            tuple(pltpu.VMEM((dbl, n, BLK), BF16) for _ in range(zn)),
            pltpu.VMEM((dn, n, BLK), BF16),
            pltpu.VMEM((max(xn - 1, 1), zn, n, BLK), BF16),
            pltpu.VMEM((2 * dbl, n, BLK), BF16),
            pltpu.VMEM((nbl + 2, n, BLK), BF16),
            pltpu.VMEM((n, width), F32),
            pltpu.VMEM(sens.shape, BF16),
            pltpu.VMEM(couple.shape, BF16),
            pltpu.VMEM(grad.shape, BF16),
            pltpu.SMEM((max(xn - 1, 1), 1, dn), jnp.int32),
            pltpu.VMEM((n, width), F32),
            pltpu.VMEM((SLICES * n, width), BF16),
            pltpu.VMEM((gn, rows, BLK), F32),
            pltpu.VMEM((gn, rows, BLK), F32),
            pltpu.VMEM((zn, rows, BLK), F32),
            pltpu.VMEM((yn, rows, BLK), F32),
            pltpu.VMEM((gn, rows, BLK), F32),
            sem((dbl + nbl + 5,)),
            sem((2, zn // 2)),
            sem((2, zn // 2)),
            sem((xn, zn)),
            sem((xn, zn)),
            sem((4,)),
            sem((4,)),
            sem((xn,)),
            sem((xn,)),
            sem((4, most)),
            sem((4, most)),
        ],
        compiler_params=pltpu.CompilerParams(
            collective_id=0, has_side_effects=True, vmem_limit_bytes=40 * 2**20
        ),
        name="gather",
    )(data, reg, prev, low, row, touched, sens, src, couple, cmap, grad, gmap)


def local(
    data_panel, reg_panel, prev_panel, lower_block, sens_tiles, sens_src, touched,
    couple_tiles, couple_map, grad_tiles, grad_map,
):
    s, g = gather(
        X_CHIPS, data_panel, reg_panel, prev_panel, lower_block, sens_tiles, sens_src, touched,
        couple_tiles, couple_map, grad_tiles, grad_map,
    )
    return finish(g, s)


def solution(mesh):
    return jax.shard_map(
        local,
        mesh=mesh,
        in_specs=(
            P(None, ("region", "dev")),
            P(None, ("region", "dev")),
            P(None, ("region", "dev")),
            P(),
            P(("region", "dev"), None, None, None),
            P(("region", "dev"), None),
            P(("region", "dev")),
            P(("region", "dev"), None, None, None),
            P(("region", "dev"), None),
            P(("region", "dev"), None, None, None),
            P(("region", "dev"), None),
        ),
        out_specs=(P(None, ("region", "dev")), P()),
        check_vma=False,
    )
```

```python
import functools

import jax
import jax.numpy as jnp
from jax import lax
from jax.experimental import pallas as pl
from jax.experimental.pallas import tpu as pltpu
from jax.sharding import PartitionSpec as P

F32 = jnp.float32
BF16 = jnp.bfloat16
SLICES = 4
BLK = 128
X_CHIPS = 4


def two_sum(a, b):
    s = a + b
    t = s - a
    return s, (a - (s - t)) + (b - t)


def cut(value, sigma):
    top = (value + sigma) - sigma
    return top, value - top


def eliminate(aug, rows):
    blocks = [aug[8 * b : 8 * b + 8, :] for b in range(rows // 8)]
    sub = lax.broadcasted_iota(jnp.int32, (8, 128), 0)
    out = []
    for b in range(rows // 8):
        live = len(blocks)
        cols = [
            [jnp.broadcast_to(blk[:, 8 * b + k : 8 * b + k + 1], (8, 128)) for blk in blocks]
            for k in range(8)
        ]
        head = blocks[0]
        pivots = jnp.ones((8, 128), F32)
        for k in range(8):
            pivot = jnp.broadcast_to(cols[k][0][k : k + 1, :], (8, 128))
            inv = 1.0 / pivot
            pivots = jnp.where(sub == k, pivot, pivots)
            factor = [c * inv for c in cols[k]]
            factor[0] = jnp.where(sub > k, factor[0], 0.0)
            for m in range(k + 1, 8):
                across = jnp.broadcast_to(cols[m][0][k : k + 1, :], (8, 128))
                cols[m] = [c - f * across for c, f in zip(cols[m], factor)]
            row = jnp.broadcast_to(head[k : k + 1, :], (8, 128))
            head = head - factor[0] * row
            blocks = [head] + [blk - f * row for blk, f in zip(blocks[1:], factor[1:])]
        root = lax.rsqrt(pivots)
        root = root * (1.5 - (0.5 * pivots) * (root * root))
        out.append(head * root)
        blocks = blocks[1:]
    return jnp.concatenate(out, axis=0)


def split3(v):
    hi = v.astype(BF16)
    r = v - hi.astype(F32)
    mid = r.astype(BF16)
    return hi, mid, (r - mid.astype(F32)).astype(BF16)


def finish_kernel(g_ref, s_any, q_ref, f_ref, s_ref, s_sem):
    n = 64
    s_copy = pltpu.make_async_copy(s_any, s_ref, s_sem)
    s_copy.start()
    g = g_ref[...]
    lane = lax.broadcasted_iota(jnp.int32, (n, 128), 1)
    subl = lax.broadcasted_iota(jnp.int32, (n, 128), 0)
    left = lane < n
    eye_right = (lane == subl + n).astype(F32)
    eye = (lane == subl).astype(F32)
    low_part = jnp.where(left, pltpu.roll(g, n, 1), 0.0)
    hi_part = jnp.where(left, g, 0.0)
    first = eliminate(hi_part + eye_right, n)

    w = jnp.where(left, pltpu.roll(first, n, 1), 0.0)
    wsig = jnp.max(jnp.abs(w), axis=1, keepdims=True) * 131072.0
    gsig = jnp.max(jnp.abs(hi_part), axis=0, keepdims=True) * 131072.0
    ws = []
    r = w
    for i in range(4):
        top, r = cut(r, wsig * (2.0 ** (-7 * i)))
        ws.append(top.astype(BF16)[:, :n])
    gs = []
    r = hi_part
    for i in range(3):
        top, r = cut(r, gsig * (2.0 ** (-7 * i)))
        gs.append(top.astype(BF16))
    r = r + low_part
    for i in range(3, 6):
        top, r = cut(r, gsig * (2.0 ** (-7 * i)))
        gs.append(top.astype(BF16))
    hi = lo = None
    for level in range(6):
        pairs = [(i, level - i) for i in range(4) if 0 <= level - i < 6]
        lhs = jnp.concatenate([ws[i] for i, _ in pairs], axis=1)
        rhs = jnp.concatenate([gs[j] for _, j in pairs], axis=0)
        term = jnp.dot(lhs, rhs, preferred_element_type=F32)
        if hi is None:
            hi, lo = term, jnp.zeros_like(term)
        else:
            hi, e = two_sum(hi, term)
            lo = lo + e
    t = hi + lo
    g2 = lax.dot_general(
        t, w, (((1,), (1,)), ((), ())), precision=lax.Precision.HIGHEST, preferred_element_type=F32
    )
    zero = jnp.zeros((n, n), F32)
    second = eliminate(jnp.concatenate([g2, zero], axis=1) + eye_right, n)
    w2 = jnp.where(left, pltpu.roll(second, n, 1), 0.0)
    both = jnp.dot(second[:, :n], first[:, :n], precision=lax.Precision.HIGHEST, preferred_element_type=F32)
    f_ref[...] = both
    m = jnp.dot(w2[:, :n], w[:, :n], precision=lax.Precision.HIGHEST, preferred_element_type=F32)
    parts = jnp.concatenate([jnp.concatenate([p] * SLICES, axis=1) for p in split3(m)], axis=0)
    s_copy.wait()
    for c in range(4):
        res = jnp.dot(parts, s_ref[:, 256 * c : 256 * c + 256], preferred_element_type=F32)
        q_ref[:, 256 * c : 256 * c + 256] = res[:n] + (res[n : 2 * n] + res[2 * n :])


def finish(g, s):
    vm = pl.BlockSpec(memory_space=pltpu.VMEM)
    return pl.pallas_call(
        finish_kernel,
        out_shape=(jax.ShapeDtypeStruct((64, 1024), F32), jax.ShapeDtypeStruct((64, 64), F32)),
        in_specs=[vm, pl.BlockSpec(memory_space=pltpu.HBM)],
        out_specs=(vm, vm),
        scratch_shapes=[pltpu.VMEM(s.shape, BF16), pltpu.SemaphoreType.DMA(())],
        compiler_params=pltpu.CompilerParams(vmem_limit_bytes=60 * 2**20),
        name="finish",
    )(g, s)


def gram_local(a):
    n = 64
    sig = jnp.max(jnp.abs(a), axis=1, keepdims=True) * 131072.0
    parts = []
    r = a
    for i in range(SLICES):
        top, r = cut(r, sig * (2.0 ** (-7 * i)))
        parts.append(top.astype(BF16))
    s = jnp.concatenate(parts, axis=0)
    p = lax.dot_general(s, s, (((1,), (1,)), ((), ())), preferred_element_type=F32)
    order = [(0, 0), (1, 0), (0, 1), (2, 0), (1, 1), (3, 0), (2, 1), (3, 1)]
    hi = lo = None
    for i, h in order:
        term = p[n * i : n * i + n, 128 * h : 128 * h + 128]
        if hi is None:
            hi, lo = term, jnp.zeros_like(term)
        else:
            hi, e = two_sum(hi, term)
            lo = lo + e
    hi, e = two_sum(hi, pltpu.roll(hi, n, 1))
    lo = (lo + pltpu.roll(lo, n, 1)) + e
    hi, lo = hi + lo, lo - ((hi + lo) - hi)
    lane = lax.broadcasted_iota(jnp.int32, (n, 128), 1)
    return s, jnp.where(lane < n, hi, pltpu.roll(lo, n, 1))


MESH = pl.DeviceIdType.MESH


def gather_kernel(
    sizes,
    data, reg, prev, low_any, touched_any, sens, src_any, couple, cmap_any, grad, gmap_any,
    s_out, g_out,
    zbs, compact, xs, side, nb, ext, prev_v, low, sens_v, couple_v, grad_v, touched, src, cmap, gmap, asked, adj, s_v, gpart, rs, zs, ys, ag,
    l_sem, z_send, z_recv, x_send, x_recv, n_send, n_recv, t_send, t_recv, a_send, a_recv,
):
    xn, zn, rn, nbl, dbl, kk, kc, kg = sizes
    n = 64
    yn, gn = rn // 2, 2 * xn
    dn = xn * zn
    rows = n // gn
    half = zn // 2
    r = lax.axis_index("region")
    d = lax.axis_index("dev")
    y, core = r // 2, r % 2
    z, x = d // xn, d % xn
    piece = x * 2 + core

    mine = zbs[0]
    below = [mine] + list(zbs[1:half])
    above = [mine] + list(zbs[half : 2 * half - 1])
    across = zbs[2 * half - 1]

    local = []

    def fetch(source, target):
        c = pltpu.make_async_copy(source, target, l_sem.at[len(local)])
        c.start()
        local.append(c)
        return c

    own = [fetch(data.at[:, pl.ds(BLK * b, BLK)], mine.at[b]) for b in range(dbl)]
    rim = [fetch(reg.at[:, pl.ds(BLK * b, BLK)], ext.at[b + 1]) for b in range(nbl)]
    maps = [fetch(a, b) for a, b in ((touched_any, touched), (src_any, src), (cmap_any, cmap), (gmap_any, gmap))]
    prev_c = fetch(prev, prev_v)
    low_c = fetch(low_any, low)
    grad_c = fetch(grad, grad_v)
    couple_c = fetch(couple, couple_v)
    sens_c = fetch(sens, sens_v)

    def group(o):
        q = (piece + o) % gn
        return (y * 2 + q % 2, z * xn + q // 2)

    def along_z(o):
        return (r, ((z + o) % zn) * xn + x)

    def along_y(o):
        return (((y + o) % yn) * 2 + core, d)

    def along_x(o):
        return (r, z * xn + (x + o) % xn)

    up, down = ((r + 1) % rn, d), ((r + rn - 1) % rn, d)
    g = r * dn + d
    g_up, g_down = (g + 1) % (rn * dn), (g + rn * dn - 1) % (rn * dn)
    after, before = (g_up // dn, g_up % dn), (g_down // dn, g_down % dn)
    reached = [group(o) for o in range(1, gn)] + [along_z(1), along_z(zn - 1)]
    reached += [along_y(o) for o in range(1, yn)] + [up, down, after, before]
    barrier = pltpu.get_barrier_semaphore()
    for who in reached:
        pl.semaphore_signal(barrier, inc=1, device_id=who, device_id_type=MESH)
    pl.semaphore_wait(barrier, len(reached))

    def remote(source, target, send, recv, who):
        c = pltpu.make_async_remote_copy(
            src_ref=source, dst_ref=target, send_sem=send, recv_sem=recv,
            device_id=who, device_id_type=MESH,
        )
        c.start()
        return c

    sent = []
    asks = []
    for o in range(1, xn):
        asks.append(remote(touched_any, asked.at[xn - o - 1], t_send.at[o - 1], t_recv.at[o - 1], along_x(o)))
    sent += asks
    def pass_on(way, step, b):
        held = (below, above)[way]
        target = held[step + 1] if step < half - 1 else across
        source = data.at[:, pl.ds(BLK * b, BLK)] if step == 0 else held[step].at[b]
        c = remote(source, target.at[b], z_send.at[way, step, b], z_recv.at[way, step, b],
                   along_z(1 if way == 0 else zn - 1))
        sent.append(c)
        moves[way, step, b] = c

    moves = {}
    x_copies = []

    def hand_on(slot, zz, held):
        for o in range(1, xn):
            xs[o - 1, slot] = held[asked[o - 1, 0, zz * xn + x]]
            x_copies.append(
                remote(xs.at[o - 1, slot], compact.at[zz * xn + x],
                       x_send.at[o - 1, slot], x_recv.at[o - 1, slot], along_x(o))
            )
        compact[zz * xn + x] = held[touched[0, zz * xn + x]]

    for b in range(dbl):
        for way in range(2):
            if half > 1 or b // (dbl // 2) == way:
                pass_on(way, 0, b)
    near = [
        remote(data, side[0], n_send.at[0], n_recv.at[0], up),
        remote(data, side[1], n_send.at[1], n_recv.at[1], down),
        remote(reg.at[:, pl.ds(BLK * (nbl - 1), BLK)], ext.at[0], n_send.at[2], n_recv.at[2], after),
        remote(reg.at[:, pl.ds(0, BLK)], ext.at[nbl + 1], n_send.at[3], n_recv.at[3], before),
    ]
    sent += near

    def gradient(first, last):
        for b in range(first, last):
            lhs = jnp.concatenate([ext[gmap[j, b]] for j in range(kg)], axis=1)
            part = jnp.dot(lhs, grad_v[b].reshape(kg * BLK, BLK), preferred_element_type=F32)
            adj[:, BLK * b : BLK * b + BLK] += 0.5 * part

    def coupling(first, last):
        for b in range(first, last):
            lhs = jnp.concatenate([nb[cmap[j, b]] for j in range(kc)], axis=1)
            part = jnp.dot(lhs, couple_v[b].reshape(kc * BLK, BLK), preferred_element_type=F32)
            adj[:, BLK * b : BLK * b + BLK] += part

    for step in range(half):
        for b in range(dbl):
            for way in range(2):
                if (way, step, b) in moves:
                    moves[way, step, b].wait_recv()
                    if step < half - 2 or (step == half - 2 and b // (dbl // 2) == way):
                        pass_on(way, step + 1, b)
        if step == 0:
            for c in own + maps:
                c.wait()
            for c in asks:
                c.wait_recv()
            hand_on(0, z, mine)
        if step < half - 1:
            hand_on(2 * step + 1, (z + zn - step - 1) % zn, below[step + 1])
            hand_on(2 * step + 2, (z + step + 1) % zn, above[step + 1])
        else:
            hand_on(zn - 1, (z + half) % zn, across)
        if step == 0:
            prev_c.wait()
            low_c.wait()
            adj[...] = -jnp.dot(
                low[...], prev_v[...], precision=lax.Precision.HIGHEST, preferred_element_type=F32
            )
        if step == min(1, half - 1):
            for c in rim:
                c.wait()
            grad_c.wait()
            couple_c.wait()
            for c in near:
                c.wait_recv()

            @pl.when(g == 0)
            def _():
                ext[0] = jnp.zeros((n, BLK), BF16)

            @pl.when(g == rn * dn - 1)
            def _():
                ext[nbl + 1] = jnp.zeros((n, BLK), BF16)

            for k, edge in ((0, 0), (1, rn - 1)):
                for b in range(dbl):
                    block = side[k][:, BLK * b : BLK * b + BLK]
                    nb[k * dbl + b] = jnp.where(r == edge, jnp.zeros_like(block), block)
            gradient(0, nbl)
            coupling(0, nbl)
    sens_c.wait()
    for c in x_copies:
        c.wait_recv()
    for b in range(nbl):
        lhs = jnp.concatenate([compact[src[b, k]] for k in range(kk)], axis=1)
        part = jnp.dot(lhs, sens_v[b].reshape(kk * BLK, BLK), preferred_element_type=F32)
        adj[:, BLK * b : BLK * b + BLK] += part

    s, gram = gram_local(adj[...])
    s_v[...] = s
    s_copy = fetch(s_v, s_out)
    gram = gram * (1.0 / (rn * dn * nbl * BLK))
    lane = lax.broadcasted_iota(jnp.int32, (n // 2, BLK), 1)
    swapped = pltpu.roll(gram, n, 1)
    top, bottom = pl.ds(0, rows // 2), pl.ds(rows // 2, rows // 2)
    gram_hi = jnp.where(lane < n, gram[: n // 2], swapped[n // 2 :])
    gram_lo = jnp.where(lane < n, swapped[: n // 2], gram[n // 2 :])
    for q in range(gn):
        part = slice(rows // 2 * q, rows // 2 * (q + 1))
        gpart[q, top] = gram_hi[part]
        gpart[q, bottom] = gram_lo[part]

    def total(ref, count, target):
        terms = [(ref[q, top], ref[q, bottom]) for q in range(count)]
        while len(terms) > 1:
            paired = []
            for (a, a_low), (b, b_low) in zip(terms[::2], terms[1::2]):
                hi, e = two_sum(a, b)
                paired.append((hi, (a_low + b_low) + e))
            terms = paired + terms[len(paired) * 2 :]
        hi, lo = terms[0]
        big = hi + lo
        target[top] = big
        target[bottom] = lo - (big - hi)

    def exchange(stage, count, mine, box, who, source):
        copies = []
        for o in range(1, count):
            copies.append(
                remote(source(o), box.at[mine], a_send.at[stage, o - 1], a_recv.at[stage, o - 1], who(o))
            )
        return copies

    copies = exchange(0, gn, piece, rs, group, lambda o: gpart.at[(piece + o) % gn])
    rs[piece] = gpart[piece]
    for c in copies:
        c.wait_recv()
    sent += copies
    total(rs, gn, zs.at[z])
    copies = exchange(1, zn, z, zs, along_z, lambda o: zs.at[z])
    for c in copies:
        c.wait_recv()
    sent += copies
    total(zs, zn, ys.at[y])
    copies = exchange(2, yn, y, ys, along_y, lambda o: ys.at[y])
    for c in copies:
        c.wait_recv()
    sent += copies
    total(ys, yn, ag.at[piece])
    copies = exchange(3, gn, piece, ag, group, lambda o: ag.at[piece])
    for c in copies:
        c.wait_recv()
    sent += copies
    hi = jnp.concatenate([ag[q, top] for q in range(gn)], axis=0)
    lo = jnp.concatenate([ag[q, bottom] for q in range(gn)], axis=0)
    g_out[: n // 2, :] = jnp.where(lane < n, hi, pltpu.roll(lo, n, 1))
    g_out[n // 2 :, :] = jnp.where(lane < n, pltpu.roll(hi, n, 1), lo)
    for c in sent + x_copies:
        c.wait_send()
    s_copy.wait()


def gather(xn, data, reg, prev, low, sens, src, touched, couple, cmap, grad, gmap):
    zn = lax.axis_size("dev") // xn
    rn = lax.axis_size("region")
    n = data.shape[0]
    nbl, kk = sens.shape[0], sens.shape[1]
    kc, kg = couple.shape[1], grad.shape[1]
    dbl = data.shape[1] // BLK
    gn, yn, dn = 2 * xn, rn // 2, xn * zn
    rows = n // gn
    most = max(gn, zn, yn) - 1
    vm = pl.BlockSpec(memory_space=pltpu.VMEM)
    hbm = pl.BlockSpec(memory_space=pltpu.HBM)
    sem = pltpu.SemaphoreType.DMA
    width = nbl * BLK
    sizes = (xn, zn, rn, nbl, dbl, kk, kc, kg)
    row = touched.reshape(1, dn)
    return pl.pallas_call(
        functools.partial(gather_kernel, sizes),
        out_shape=(
            jax.ShapeDtypeStruct((SLICES * n, width), BF16),
            jax.ShapeDtypeStruct((n, BLK), F32),
        ),
        in_specs=[hbm] * 11,
        out_specs=(hbm, vm),
        scratch_shapes=[
            tuple(pltpu.VMEM((dbl, n, BLK), BF16) for _ in range(zn)),
            pltpu.VMEM((dn, n, BLK), BF16),
            pltpu.VMEM((max(xn - 1, 1), zn, n, BLK), BF16),
            tuple(pltpu.VMEM((n, dbl * BLK), BF16) for _ in range(2)),
            pltpu.VMEM((2 * dbl, n, BLK), BF16),
            pltpu.VMEM((nbl + 2, n, BLK), BF16),
            pltpu.VMEM((n, width), F32),
            pltpu.VMEM((n, n), F32),
            pltpu.VMEM(sens.shape, BF16),
            pltpu.VMEM(couple.shape, BF16),
            pltpu.VMEM(grad.shape, BF16),
            pltpu.SMEM((1, dn), jnp.int32),
            pltpu.SMEM((nbl, kk), jnp.int32),
            pltpu.SMEM((kc, nbl), jnp.int32),
            pltpu.SMEM((kg, nbl), jnp.int32),
            pltpu.SMEM((max(xn - 1, 1), 1, dn), jnp.int32),
            pltpu.VMEM((n, width), F32),
            pltpu.VMEM((SLICES * n, width), BF16),
            pltpu.VMEM((gn, rows, BLK), F32),
            pltpu.VMEM((gn, rows, BLK), F32),
            pltpu.VMEM((zn, rows, BLK), F32),
            pltpu.VMEM((yn, rows, BLK), F32),
            pltpu.VMEM((gn, rows, BLK), F32),
            sem((dbl + nbl + 10,)),
            sem((2, zn // 2, dbl)),
            sem((2, zn // 2, dbl)),
            sem((xn, zn)),
            sem((xn, zn)),
            sem((4,)),
            sem((4,)),
            sem((xn,)),
            sem((xn,)),
            sem((4, most)),
            sem((4, most)),
        ],
        compiler_params=pltpu.CompilerParams(
            collective_id=0, has_side_effects=True, vmem_limit_bytes=60 * 2**20
        ),
        name="gather",
    )(data, reg, prev, low, row, sens, src, couple, cmap.T, grad, gmap.T)


def local(
    data_panel, reg_panel, prev_panel, lower_block, sens_tiles, sens_src, touched,
    couple_tiles, couple_map, grad_tiles, grad_map,
):
    s, g = gather(
        X_CHIPS, data_panel, reg_panel, prev_panel, lower_block, sens_tiles, sens_src, touched,
        couple_tiles, couple_map, grad_tiles, grad_map,
    )
    return finish(g, s)


def solution(mesh):
    return jax.shard_map(
        local,
        mesh=mesh,
        in_specs=(
            P(None, ("region", "dev")),
            P(None, ("region", "dev")),
            P(None, ("region", "dev")),
            P(),
            P(("region", "dev"), None, None, None),
            P(("region", "dev"), None),
            P(("region", "dev")),
            P(("region", "dev"), None, None, None),
            P(("region", "dev"), None),
            P(("region", "dev"), None, None, None),
            P(("region", "dev"), None),
        ),
        out_specs=(P(None, ("region", "dev")), P()),
        check_vma=False,
    )
```

```python
import functools

import jax
import jax.numpy as jnp
from jax import lax
from jax.experimental import pallas as pl
from jax.experimental.pallas import tpu as pltpu
from jax.sharding import PartitionSpec as P

F32 = jnp.float32
BF16 = jnp.bfloat16
SLICES = 4
BLK = 128
X_CHIPS = 4


def two_sum(a, b):
    s = a + b
    t = s - a
    return s, (a - (s - t)) + (b - t)


def cut(value, sigma):
    top = (value + sigma) - sigma
    return top, value - top


def eliminate(aug, rows):
    blocks = [aug[8 * b : 8 * b + 8, :] for b in range(rows // 8)]
    sub = lax.broadcasted_iota(jnp.int32, (8, 128), 0)
    out = []
    for b in range(rows // 8):
        live = len(blocks)
        cols = [
            [jnp.broadcast_to(blk[:, 8 * b + k : 8 * b + k + 1], (8, 128)) for blk in blocks]
            for k in range(8)
        ]
        head = blocks[0]
        pivots = jnp.ones((8, 128), F32)
        for k in range(8):
            pivot = jnp.broadcast_to(cols[k][0][k : k + 1, :], (8, 128))
            inv = 1.0 / pivot
            pivots = jnp.where(sub == k, pivot, pivots)
            factor = [c * inv for c in cols[k]]
            factor[0] = jnp.where(sub > k, factor[0], 0.0)
            for m in range(k + 1, 8):
                across = jnp.broadcast_to(cols[m][0][k : k + 1, :], (8, 128))
                cols[m] = [c - f * across for c, f in zip(cols[m], factor)]
            row = jnp.broadcast_to(head[k : k + 1, :], (8, 128))
            head = head - factor[0] * row
            blocks = [head] + [blk - f * row for blk, f in zip(blocks[1:], factor[1:])]
        root = lax.rsqrt(pivots)
        root = root * (1.5 - (0.5 * pivots) * (root * root))
        out.append(head * root)
        blocks = blocks[1:]
    return jnp.concatenate(out, axis=0)


def split3(v):
    hi = v.astype(BF16)
    r = v - hi.astype(F32)
    mid = r.astype(BF16)
    return hi, mid, (r - mid.astype(F32)).astype(BF16)


def finish_kernel(g_ref, s_ref, q_ref, f_ref):
    n = 64
    g = g_ref[...]
    lane = lax.broadcasted_iota(jnp.int32, (n, 128), 1)
    subl = lax.broadcasted_iota(jnp.int32, (n, 128), 0)
    left = lane < n
    eye_right = (lane == subl + n).astype(F32)
    eye = (lane == subl).astype(F32)
    low_part = jnp.where(left, pltpu.roll(g, n, 1), 0.0)
    hi_part = jnp.where(left, g, 0.0)
    first = eliminate(hi_part + eye_right, n)

    w = jnp.where(left, pltpu.roll(first, n, 1), 0.0)
    wsig = jnp.max(jnp.abs(w), axis=1, keepdims=True) * 131072.0
    gsig = jnp.max(jnp.abs(hi_part), axis=0, keepdims=True) * 131072.0
    ws = []
    r = w
    for i in range(4):
        top, r = cut(r, wsig * (2.0 ** (-7 * i)))
        ws.append(top.astype(BF16)[:, :n])
    gs = []
    r = hi_part
    for i in range(3):
        top, r = cut(r, gsig * (2.0 ** (-7 * i)))
        gs.append(top.astype(BF16))
    r = r + low_part
    for i in range(3, 6):
        top, r = cut(r, gsig * (2.0 ** (-7 * i)))
        gs.append(top.astype(BF16))
    hi = lo = None
    for level in range(6):
        pairs = [(i, level - i) for i in range(4) if 0 <= level - i < 6]
        lhs = jnp.concatenate([ws[i] for i, _ in pairs], axis=1)
        rhs = jnp.concatenate([gs[j] for _, j in pairs], axis=0)
        term = jnp.dot(lhs, rhs, preferred_element_type=F32)
        if hi is None:
            hi, lo = term, jnp.zeros_like(term)
        else:
            hi, e = two_sum(hi, term)
            lo = lo + e
    t = hi + lo
    g2 = lax.dot_general(
        t, w, (((1,), (1,)), ((), ())), precision=lax.Precision.HIGHEST, preferred_element_type=F32
    )
    zero = jnp.zeros((n, n), F32)
    second = eliminate(jnp.concatenate([g2, zero], axis=1) + eye_right, n)
    w2 = jnp.where(left, pltpu.roll(second, n, 1), 0.0)
    both = jnp.dot(second[:, :n], first[:, :n], precision=lax.Precision.HIGHEST, preferred_element_type=F32)
    f_ref[...] = both
    m = jnp.dot(w2[:, :n], w[:, :n], precision=lax.Precision.HIGHEST, preferred_element_type=F32)
    parts = jnp.concatenate([jnp.concatenate([p] * SLICES, axis=1) for p in split3(m)], axis=0)
    for c in range(4):
        res = jnp.dot(parts, s_ref[:, 256 * c : 256 * c + 256], preferred_element_type=F32)
        q_ref[:, 256 * c : 256 * c + 256] = res[:n] + (res[n : 2 * n] + res[2 * n :])


def finish(g, s):
    vm = pl.BlockSpec(memory_space=pltpu.VMEM)
    return pl.pallas_call(
        finish_kernel,
        out_shape=(jax.ShapeDtypeStruct((64, 1024), F32), jax.ShapeDtypeStruct((64, 64), F32)),
        in_specs=[vm, vm],
        out_specs=(vm, vm),
        compiler_params=pltpu.CompilerParams(vmem_limit_bytes=32 * 2**20),
        name="finish",
    )(g, s)


def gram_local(a):
    n = 64
    sig = jnp.max(jnp.abs(a), axis=1, keepdims=True) * 131072.0
    parts = []
    r = a
    for i in range(SLICES):
        top, r = cut(r, sig * (2.0 ** (-7 * i)))
        parts.append(top.astype(BF16))
    s = jnp.concatenate(parts, axis=0)
    p = lax.dot_general(s, s, (((1,), (1,)), ((), ())), preferred_element_type=F32)
    order = [(0, 0), (1, 0), (0, 1), (2, 0), (1, 1), (3, 0), (2, 1), (3, 1)]
    hi = lo = None
    for i, h in order:
        term = p[n * i : n * i + n, 128 * h : 128 * h + 128]
        if hi is None:
            hi, lo = term, jnp.zeros_like(term)
        else:
            hi, e = two_sum(hi, term)
            lo = lo + e
    hi, e = two_sum(hi, pltpu.roll(hi, n, 1))
    lo = (lo + pltpu.roll(lo, n, 1)) + e
    hi, lo = hi + lo, lo - ((hi + lo) - hi)
    lane = lax.broadcasted_iota(jnp.int32, (n, 128), 1)
    return s, jnp.where(lane < n, hi, pltpu.roll(lo, n, 1))


MESH = pl.DeviceIdType.MESH


def gather_kernel(
    sizes,
    data, reg, prev, low_any, touched_any, sens, src_any, couple, cmap_any, grad, gmap_any,
    s_out, g_out,
    zbs, compact, xs, side, nb, ext, prev_v, low, sens_v, couple_v, grad_v, touched, src, cmap, gmap, asked, adj, gpart, rs, zs, ys, ag,
    l_sem, z_send, z_recv, x_send, x_recv, n_send, n_recv, t_send, t_recv, a_send, a_recv,
):
    xn, zn, rn, nbl, dbl, kk, kc, kg = sizes
    n = 64
    yn, gn = rn // 2, 2 * xn
    dn = xn * zn
    rows = n // gn
    half = zn // 2
    r = lax.axis_index("region")
    d = lax.axis_index("dev")
    y, core = r // 2, r % 2
    z, x = d // xn, d % xn
    piece = x * 2 + core

    mine = zbs[0]
    below = [mine] + list(zbs[1:half])
    above = [mine] + list(zbs[half : 2 * half - 1])
    across = zbs[2 * half - 1]

    def group(o):
        q = (piece + o) % gn
        return (y * 2 + q % 2, z * xn + q // 2)

    def along_z(o):
        return (r, ((z + o) % zn) * xn + x)

    def along_y(o):
        return (((y + o) % yn) * 2 + core, d)

    def along_x(o):
        return (r, z * xn + (x + o) % xn)

    up, down = ((r + 1) % rn, d), ((r + rn - 1) % rn, d)
    g = r * dn + d
    g_up, g_down = (g + 1) % (rn * dn), (g + rn * dn - 1) % (rn * dn)
    after, before = (g_up // dn, g_up % dn), (g_down // dn, g_down % dn)
    reached = [group(o) for o in range(1, gn)] + [along_z(o) for o in range(1, zn) if min(o, zn - o) <= 2]
    reached += [along_y(o) for o in range(1, yn)] + [up, down, after, before]
    barrier = pltpu.get_barrier_semaphore()
    for who in reached:
        pl.semaphore_signal(barrier, inc=1, device_id=who, device_id_type=MESH)
    local = []

    def fetch(source, target):
        c = pltpu.make_async_copy(source, target, l_sem.at[len(local)])
        c.start()
        local.append(c)
        return c

    own = [fetch(data.at[:, pl.ds(BLK * b, BLK)], mine.at[b]) for b in range(dbl)]
    rim = [fetch(reg.at[:, pl.ds(BLK * b, BLK)], ext.at[b + 1]) for b in range(nbl)]
    maps = [fetch(a, b) for a, b in ((touched_any, touched), (src_any, src), (cmap_any, cmap), (gmap_any, gmap))]
    prev_c = fetch(prev, prev_v)
    low_c = fetch(low_any, low)
    grad_c = fetch(grad, grad_v)
    couple_c = fetch(couple, couple_v)
    sens_c = fetch(sens, sens_v)

    pl.semaphore_wait(barrier, len(reached))

    def remote(source, target, send, recv, who):
        c = pltpu.make_async_remote_copy(
            src_ref=source, dst_ref=target, send_sem=send, recv_sem=recv,
            device_id=who, device_id_type=MESH,
        )
        c.start()
        return c

    sent = []
    asks = []
    for o in range(1, xn):
        asks.append(remote(touched_any, asked.at[xn - o - 1], t_send.at[o - 1], t_recv.at[o - 1], along_x(o)))
    sent += asks
    def pass_on(way, far, b):
        held = (below, above)[way]
        target = held[far] if far < half else across
        hops = far if far <= 2 else far - 2
        source = (mine if far <= 2 else held[2]).at[b]
        c = remote(source, target.at[b], z_send.at[way, far - 1, b], z_recv.at[way, far - 1, b],
                   along_z(hops if way == 0 else zn - hops))
        sent.append(c)
        moves[way, far, b] = c

    def parts(far):
        return [(way, b) for b in range(dbl) for way in range(2) if far < half or b // (dbl // 2) == way]

    moves = {}
    x_copies = []

    def hand_on(slot, zz, held):
        for o in range(1, xn):
            xs[o - 1, slot] = held[asked[o - 1, 0, zz * xn + x]]
            x_copies.append(
                remote(xs.at[o - 1, slot], compact.at[zz * xn + x],
                       x_send.at[o - 1, slot], x_recv.at[o - 1, slot], along_x(o))
            )
        compact[zz * xn + x] = held[touched[0, zz * xn + x]]

    for c in own:
        c.wait()
    for far in range(min(2, half), 0, -1):
        for way, b in parts(far):
            pass_on(way, far, b)
    near = [
        remote(data, side[0], n_send.at[0], n_recv.at[0], up),
        remote(data, side[1], n_send.at[1], n_recv.at[1], down),
        remote(reg.at[:, pl.ds(BLK * (nbl - 1), BLK)], ext.at[0], n_send.at[2], n_recv.at[2], after),
        remote(reg.at[:, pl.ds(0, BLK)], ext.at[nbl + 1], n_send.at[3], n_recv.at[3], before),
    ]
    sent += near

    def gradient(first, last):
        for b in range(first, last):
            lhs = jnp.concatenate([ext[gmap[j, b]] for j in range(kg)], axis=1)
            part = jnp.dot(lhs, grad_v[b].reshape(kg * BLK, BLK), preferred_element_type=F32)
            adj[:, BLK * b : BLK * b + BLK] += 0.5 * part

    def coupling(first, last):
        for b in range(first, last):
            lhs = jnp.concatenate([nb[cmap[j, b]] for j in range(kc)], axis=1)
            part = jnp.dot(lhs, couple_v[b].reshape(kc * BLK, BLK), preferred_element_type=F32)
            adj[:, BLK * b : BLK * b + BLK] += part

    def arrive(far):
        for way, b in parts(far):
            moves[way, far, b].wait_recv()
            if far == 2:
                for further in range(half, 2, -1):
                    if (way, b) in parts(further):
                        pass_on(way, further, b)

    def hand_on_far(far):
        if far < half:
            hand_on(2 * far - 1, (z + zn - far) % zn, below[far])
            hand_on(2 * far, (z + far) % zn, above[far])
        else:
            hand_on(zn - 1, (z + half) % zn, across)

    for far in range(min(2, half), 0, -1):
        arrive(far)
    for c in maps:
        c.wait()
    for c in asks:
        c.wait_recv()
    hand_on(0, z, mine)
    for far in range(1, min(2, half) + 1):
        hand_on_far(far)
    prev_c.wait()
    low_c.wait()
    adj[...] = -jnp.dot(
        low[...], prev_v[...], precision=lax.Precision.HIGHEST, preferred_element_type=F32
    )
    for c in rim:
        c.wait()
    grad_c.wait()
    couple_c.wait()
    for c in near:
        c.wait_recv()

    @pl.when(g == 0)
    def _():
        ext[0] = jnp.zeros((n, BLK), BF16)

    @pl.when(g == rn * dn - 1)
    def _():
        ext[nbl + 1] = jnp.zeros((n, BLK), BF16)

    for k, edge in ((0, 0), (1, rn - 1)):
        for b in range(dbl):
            block = side[k][:, BLK * b : BLK * b + BLK]
            nb[k * dbl + b] = jnp.where(r == edge, jnp.zeros_like(block), block)
    gradient(0, nbl)
    coupling(0, nbl)
    for far in range(3, half + 1):
        arrive(far)
        hand_on_far(far)
    sens_c.wait()
    for c in x_copies:
        c.wait_recv()
    for b in range(nbl):
        lhs = jnp.concatenate([compact[src[b, k]] for k in range(kk)], axis=1)
        part = jnp.dot(lhs, sens_v[b].reshape(kk * BLK, BLK), preferred_element_type=F32)
        adj[:, BLK * b : BLK * b + BLK] += part

    s, gram = gram_local(adj[...])
    s_out[...] = s
    gram = gram * (1.0 / (rn * dn * nbl * BLK))
    lane = lax.broadcasted_iota(jnp.int32, (n // 2, BLK), 1)
    swapped = pltpu.roll(gram, n, 1)
    top, bottom = pl.ds(0, rows // 2), pl.ds(rows // 2, rows // 2)
    gram_hi = jnp.where(lane < n, gram[: n // 2], swapped[n // 2 :])
    gram_lo = jnp.where(lane < n, swapped[: n // 2], gram[n // 2 :])
    for q in range(gn):
        part = slice(rows // 2 * q, rows // 2 * (q + 1))
        gpart[q, top] = gram_hi[part]
        gpart[q, bottom] = gram_lo[part]

    def total(ref, count, target):
        terms = [(ref[q, top], ref[q, bottom]) for q in range(count)]
        while len(terms) > 1:
            paired = []
            for (a, a_low), (b, b_low) in zip(terms[::2], terms[1::2]):
                hi, e = two_sum(a, b)
                paired.append((hi, (a_low + b_low) + e))
            terms = paired + terms[len(paired) * 2 :]
        hi, lo = terms[0]
        big = hi + lo
        target[top] = big
        target[bottom] = lo - (big - hi)

    def exchange(stage, count, mine, box, who, source):
        copies = []
        for o in range(1, count):
            copies.append(
                remote(source(o), box.at[mine], a_send.at[stage, o - 1], a_recv.at[stage, o - 1], who(o))
            )
        return copies

    copies = exchange(0, gn, piece, rs, group, lambda o: gpart.at[(piece + o) % gn])
    rs[piece] = gpart[piece]
    for c in copies:
        c.wait_recv()
    sent += copies
    total(rs, gn, zs.at[z])
    copies = exchange(1, zn, z, zs, along_z, lambda o: zs.at[z])
    for c in copies:
        c.wait_recv()
    sent += copies
    total(zs, zn, ys.at[y])
    copies = exchange(2, yn, y, ys, along_y, lambda o: ys.at[y])
    for c in copies:
        c.wait_recv()
    sent += copies
    total(ys, yn, ag.at[piece])
    copies = exchange(3, gn, piece, ag, group, lambda o: ag.at[piece])
    for c in copies:
        c.wait_recv()
    sent += copies
    hi = jnp.concatenate([ag[q, top] for q in range(gn)], axis=0)
    lo = jnp.concatenate([ag[q, bottom] for q in range(gn)], axis=0)
    g_out[: n // 2, :] = jnp.where(lane < n, hi, pltpu.roll(lo, n, 1))
    g_out[n // 2 :, :] = jnp.where(lane < n, pltpu.roll(hi, n, 1), lo)
    for c in sent + x_copies:
        c.wait_send()


def gather(xn, data, reg, prev, low, sens, src, touched, couple, cmap, grad, gmap):
    zn = lax.axis_size("dev") // xn
    rn = lax.axis_size("region")
    n = data.shape[0]
    nbl, kk = sens.shape[0], sens.shape[1]
    kc, kg = couple.shape[1], grad.shape[1]
    dbl = data.shape[1] // BLK
    gn, yn, dn = 2 * xn, rn // 2, xn * zn
    rows = n // gn
    most = max(gn, zn, yn) - 1
    vm = pl.BlockSpec(memory_space=pltpu.VMEM)
    hbm = pl.BlockSpec(memory_space=pltpu.HBM)
    sem = pltpu.SemaphoreType.DMA
    width = nbl * BLK
    sizes = (xn, zn, rn, nbl, dbl, kk, kc, kg)
    row = touched.reshape(1, dn)
    return pl.pallas_call(
        functools.partial(gather_kernel, sizes),
        out_shape=(
            pltpu.VMEM((SLICES * n, width), BF16),
            pltpu.VMEM((n, BLK), F32),
        ),
        in_specs=[hbm] * 11,
        out_specs=(vm, vm),
        scratch_shapes=[
            tuple(pltpu.VMEM((dbl, n, BLK), BF16) for _ in range(zn)),
            pltpu.VMEM((dn, n, BLK), BF16),
            pltpu.VMEM((max(xn - 1, 1), zn, n, BLK), BF16),
            tuple(pltpu.VMEM((n, dbl * BLK), BF16) for _ in range(2)),
            pltpu.VMEM((2 * dbl, n, BLK), BF16),
            pltpu.VMEM((nbl + 2, n, BLK), BF16),
            pltpu.VMEM((n, width), F32),
            pltpu.VMEM((n, n), F32),
            pltpu.VMEM(sens.shape, BF16),
            pltpu.VMEM(couple.shape, BF16),
            pltpu.VMEM(grad.shape, BF16),
            pltpu.SMEM((1, dn), jnp.int32),
            pltpu.SMEM((nbl, kk), jnp.int32),
            pltpu.SMEM((kc, nbl), jnp.int32),
            pltpu.SMEM((kg, nbl), jnp.int32),
            pltpu.SMEM((max(xn - 1, 1), 1, dn), jnp.int32),
            pltpu.VMEM((n, width), F32),
            pltpu.VMEM((gn, rows, BLK), F32),
            pltpu.VMEM((gn, rows, BLK), F32),
            pltpu.VMEM((zn, rows, BLK), F32),
            pltpu.VMEM((yn, rows, BLK), F32),
            pltpu.VMEM((gn, rows, BLK), F32),
            sem((dbl + nbl + 10,)),
            sem((2, zn // 2, dbl)),
            sem((2, zn // 2, dbl)),
            sem((xn, zn)),
            sem((xn, zn)),
            sem((4,)),
            sem((4,)),
            sem((xn,)),
            sem((xn,)),
            sem((4, most)),
            sem((4, most)),
        ],
        compiler_params=pltpu.CompilerParams(
            collective_id=0, has_side_effects=True, vmem_limit_bytes=60 * 2**20
        ),
        name="gather",
    )(data, reg, prev, low, row, sens, src, couple, cmap.T, grad, gmap.T)


def local(
    data_panel, reg_panel, prev_panel, lower_block, sens_tiles, sens_src, touched,
    couple_tiles, couple_map, grad_tiles, grad_map,
):
    s, g = gather(
        X_CHIPS, data_panel, reg_panel, prev_panel, lower_block, sens_tiles, sens_src, touched,
        couple_tiles, couple_map, grad_tiles, grad_map,
    )
    return finish(g, s)


def solution(mesh):
    return jax.shard_map(
        local,
        mesh=mesh,
        in_specs=(
            P(None, ("region", "dev")),
            P(None, ("region", "dev")),
            P(None, ("region", "dev")),
            P(),
            P(("region", "dev"), None, None, None),
            P(("region", "dev"), None),
            P(("region", "dev")),
            P(("region", "dev"), None, None, None),
            P(("region", "dev"), None),
            P(("region", "dev"), None, None, None),
            P(("region", "dev"), None),
        ),
        out_specs=(P(None, ("region", "dev")), P()),
        check_vma=False,
    )
```

```python
import functools

import jax
import jax.numpy as jnp
from jax import lax
from jax.experimental import pallas as pl
from jax.experimental.pallas import tpu as pltpu
from jax.sharding import PartitionSpec as P

F32 = jnp.float32
BF16 = jnp.bfloat16
SLICES = 4
BLK = 128
X_CHIPS = 4


def two_sum(a, b):
    s = a + b
    t = s - a
    return s, (a - (s - t)) + (b - t)


def cut(value, sigma):
    top = (value + sigma) - sigma
    return top, value - top


def eliminate(aug, rows):
    blocks = [aug[8 * b : 8 * b + 8, :] for b in range(rows // 8)]
    sub = lax.broadcasted_iota(jnp.int32, (8, 128), 0)
    out = []
    for b in range(rows // 8):
        live = len(blocks)
        cols = [
            [jnp.broadcast_to(blk[:, 8 * b + k : 8 * b + k + 1], (8, 128)) for blk in blocks]
            for k in range(8)
        ]
        head = blocks[0]
        pivots = jnp.ones((8, 128), F32)
        for k in range(8):
            pivot = jnp.broadcast_to(cols[k][0][k : k + 1, :], (8, 128))
            inv = 1.0 / pivot
            pivots = jnp.where(sub == k, pivot, pivots)
            factor = [c * inv for c in cols[k]]
            factor[0] = jnp.where(sub > k, factor[0], 0.0)
            for m in range(k + 1, 8):
                across = jnp.broadcast_to(cols[m][0][k : k + 1, :], (8, 128))
                cols[m] = [c - f * across for c, f in zip(cols[m], factor)]
            row = jnp.broadcast_to(head[k : k + 1, :], (8, 128))
            head = head - factor[0] * row
            blocks = [head] + [blk - f * row for blk, f in zip(blocks[1:], factor[1:])]
        root = lax.rsqrt(pivots)
        root = root * (1.5 - (0.5 * pivots) * (root * root))
        out.append(head * root)
        blocks = blocks[1:]
    return jnp.concatenate(out, axis=0)


def split3(v):
    hi = v.astype(BF16)
    r = v - hi.astype(F32)
    mid = r.astype(BF16)
    return hi, mid, (r - mid.astype(F32)).astype(BF16)


def finish_kernel(g_ref, s_ref, q_ref, f_ref):
    n = 64
    g = g_ref[...]
    lane = lax.broadcasted_iota(jnp.int32, (n, 128), 1)
    subl = lax.broadcasted_iota(jnp.int32, (n, 128), 0)
    left = lane < n
    eye_right = (lane == subl + n).astype(F32)
    eye = (lane == subl).astype(F32)
    low_part = jnp.where(left, pltpu.roll(g, n, 1), 0.0)
    hi_part = jnp.where(left, g, 0.0)
    first = eliminate(hi_part + eye_right, n)

    w = jnp.where(left, pltpu.roll(first, n, 1), 0.0)
    wsig = jnp.max(jnp.abs(w), axis=1, keepdims=True) * 131072.0
    gsig = jnp.max(jnp.abs(hi_part), axis=0, keepdims=True) * 131072.0
    ws = []
    r = w
    for i in range(4):
        top, r = cut(r, wsig * (2.0 ** (-7 * i)))
        ws.append(top.astype(BF16)[:, :n])
    gs = []
    r = hi_part
    for i in range(3):
        top, r = cut(r, gsig * (2.0 ** (-7 * i)))
        gs.append(top.astype(BF16))
    r = r + low_part
    for i in range(3, 6):
        top, r = cut(r, gsig * (2.0 ** (-7 * i)))
        gs.append(top.astype(BF16))
    hi = lo = None
    for level in range(6):
        pairs = [(i, level - i) for i in range(4) if 0 <= level - i < 6]
        lhs = jnp.concatenate([ws[i] for i, _ in pairs], axis=1)
        rhs = jnp.concatenate([gs[j] for _, j in pairs], axis=0)
        term = jnp.dot(lhs, rhs, preferred_element_type=F32)
        if hi is None:
            hi, lo = term, jnp.zeros_like(term)
        else:
            hi, e = two_sum(hi, term)
            lo = lo + e
    t = hi + lo
    g2 = lax.dot_general(
        t, w, (((1,), (1,)), ((), ())), precision=lax.Precision.HIGHEST, preferred_element_type=F32
    )
    zero = jnp.zeros((n, n), F32)
    second = eliminate(jnp.concatenate([g2, zero], axis=1) + eye_right, n)
    w2 = jnp.where(left, pltpu.roll(second, n, 1), 0.0)
    both = jnp.dot(second[:, :n], first[:, :n], precision=lax.Precision.HIGHEST, preferred_element_type=F32)
    f_ref[...] = both
    m = jnp.dot(w2[:, :n], w[:, :n], precision=lax.Precision.HIGHEST, preferred_element_type=F32)
    parts = jnp.concatenate([jnp.concatenate([p] * SLICES, axis=1) for p in split3(m)], axis=0)
    for c in range(4):
        res = jnp.dot(parts, s_ref[:, 256 * c : 256 * c + 256], preferred_element_type=F32)
        q_ref[:, 256 * c : 256 * c + 256] = res[:n] + (res[n : 2 * n] + res[2 * n :])


def finish(g, s):
    vm = pl.BlockSpec(memory_space=pltpu.VMEM)
    return pl.pallas_call(
        finish_kernel,
        out_shape=(jax.ShapeDtypeStruct((64, 1024), F32), jax.ShapeDtypeStruct((64, 64), F32)),
        in_specs=[vm, vm],
        out_specs=(vm, vm),
        compiler_params=pltpu.CompilerParams(vmem_limit_bytes=32 * 2**20),
        name="finish",
    )(g, s)


def gram_local(a):
    n = 64
    sig = jnp.max(jnp.abs(a), axis=1, keepdims=True) * 131072.0
    parts = []
    r = a
    for i in range(SLICES):
        top, r = cut(r, sig * (2.0 ** (-7 * i)))
        parts.append(top.astype(BF16))
    s = jnp.concatenate(parts, axis=0)
    p = lax.dot_general(s, s, (((1,), (1,)), ((), ())), preferred_element_type=F32)
    order = [(0, 0), (1, 0), (0, 1), (2, 0), (1, 1), (3, 0), (2, 1), (3, 1)]
    hi = lo = None
    for i, h in order:
        term = p[n * i : n * i + n, 128 * h : 128 * h + 128]
        if hi is None:
            hi, lo = term, jnp.zeros_like(term)
        else:
            hi, e = two_sum(hi, term)
            lo = lo + e
    hi, e = two_sum(hi, pltpu.roll(hi, n, 1))
    lo = (lo + pltpu.roll(lo, n, 1)) + e
    hi, lo = hi + lo, lo - ((hi + lo) - hi)
    lane = lax.broadcasted_iota(jnp.int32, (n, 128), 1)
    return s, jnp.where(lane < n, hi, pltpu.roll(lo, n, 1))


MESH = pl.DeviceIdType.MESH


def gather_kernel(
    sizes,
    data, reg, prev, low_any, touched_any, sens, src_any, couple, cmap_any, grad, gmap_any,
    s_out, g_out,
    zbs, compact, xs, side, nb, ext, prev_v, low, sens_v, couple_v, grad_v, touched, src, cmap, gmap, asked, adj, gpart, rs, zs, ys, ag,
    l_sem, z_send, z_recv, x_send, x_recv, n_send, n_recv, t_send, t_recv, a_send, a_recv,
):
    xn, zn, rn, nbl, dbl, kk, kc, kg = sizes
    n = 64
    yn, gn = rn // 2, 2 * xn
    dn = xn * zn
    rows = n // gn
    half = zn // 2
    r = lax.axis_index("region")
    d = lax.axis_index("dev")
    y, core = r // 2, r % 2
    z, x = d // xn, d % xn
    piece = x * 2 + core

    mine = zbs[0]
    below = [mine] + list(zbs[1:half])
    above = [mine] + list(zbs[half : 2 * half - 1])
    across = zbs[2 * half - 1]

    local = []

    def fetch(source, target):
        c = pltpu.make_async_copy(source, target, l_sem.at[len(local)])
        c.start()
        local.append(c)
        return c

    own = [fetch(data.at[:, pl.ds(BLK * b, BLK)], mine.at[b]) for b in range(dbl)]
    maps = [fetch(a, b) for a, b in ((touched_any, touched), (src_any, src), (cmap_any, cmap), (gmap_any, gmap))]
    def group(o):
        q = (piece + o) % gn
        return (y * 2 + q % 2, z * xn + q // 2)

    def along_z(o):
        return (r, ((z + o) % zn) * xn + x)

    def along_y(o):
        return (((y + o) % yn) * 2 + core, d)

    def along_x(o):
        return (r, z * xn + (x + o) % xn)

    up, down = ((r + 1) % rn, d), ((r + rn - 1) % rn, d)
    g = r * dn + d
    g_up, g_down = (g + 1) % (rn * dn), (g + rn * dn - 1) % (rn * dn)
    after, before = (g_up // dn, g_up % dn), (g_down // dn, g_down % dn)
    reached = [group(o) for o in range(1, gn)] + [along_z(o) for o in range(1, zn) if min(o, zn - o) <= 2]
    reached += [along_y(o) for o in range(1, yn)] + [up, down, after, before]
    barrier = pltpu.get_barrier_semaphore()
    for who in reached:
        pl.semaphore_signal(barrier, inc=1, device_id=who, device_id_type=MESH)
    pl.semaphore_wait(barrier, len(reached))

    def remote(source, target, send, recv, who):
        c = pltpu.make_async_remote_copy(
            src_ref=source, dst_ref=target, send_sem=send, recv_sem=recv,
            device_id=who, device_id_type=MESH,
        )
        c.start()
        return c

    sent = []
    asks = []
    for o in range(1, xn):
        asks.append(remote(touched_any, asked.at[xn - o - 1], t_send.at[o - 1], t_recv.at[o - 1], along_x(o)))
    sent += asks
    def pass_on(way, far, b):
        held = (below, above)[way]
        target = held[far] if far < half else across
        hops = far if far <= 2 else far - 2
        source = (mine if far <= 2 else held[2]).at[b]
        c = remote(source, target.at[b], z_send.at[way, far - 1, b], z_recv.at[way, far - 1, b],
                   along_z(hops if way == 0 else zn - hops))
        sent.append(c)
        moves[way, far, b] = c

    def parts(far):
        return [(way, b) for b in range(dbl) for way in range(2) if far < half or b // (dbl // 2) == way]

    moves = {}
    x_copies = []

    def hand_on(slot, zz, held):
        for o in range(1, xn):
            xs[o - 1, slot] = held[asked[o - 1, 0, zz * xn + x]]
            x_copies.append(
                remote(xs.at[o - 1, slot], compact.at[zz * xn + x],
                       x_send.at[o - 1, slot], x_recv.at[o - 1, slot], along_x(o))
            )
        compact[zz * xn + x] = held[touched[0, zz * xn + x]]

    for c in own:
        c.wait()
    for far in range(min(2, half), 0, -1):
        for way, b in parts(far):
            pass_on(way, far, b)
    near = [
        remote(data, side[0], n_send.at[0], n_recv.at[0], up),
        remote(data, side[1], n_send.at[1], n_recv.at[1], down),
        remote(reg.at[:, pl.ds(BLK * (nbl - 1), BLK)], ext.at[0], n_send.at[2], n_recv.at[2], after),
        remote(reg.at[:, pl.ds(0, BLK)], ext.at[nbl + 1], n_send.at[3], n_recv.at[3], before),
    ]
    sent += near

    def gradient(first, last):
        for b in range(first, last):
            lhs = jnp.concatenate([ext[gmap[j, b]] for j in range(kg)], axis=1)
            part = jnp.dot(lhs, grad_v[b].reshape(kg * BLK, BLK), preferred_element_type=F32)
            adj[:, BLK * b : BLK * b + BLK] += 0.5 * part

    def coupling(first, last):
        for b in range(first, last):
            lhs = jnp.concatenate([nb[cmap[j, b]] for j in range(kc)], axis=1)
            part = jnp.dot(lhs, couple_v[b].reshape(kc * BLK, BLK), preferred_element_type=F32)
            adj[:, BLK * b : BLK * b + BLK] += part

    def arrive(far):
        for way, b in parts(far):
            moves[way, far, b].wait_recv()
            if far == 2:
                for further in range(half, 2, -1):
                    if (way, b) in parts(further):
                        pass_on(way, further, b)

    def hand_on_far(far):
        if far < half:
            hand_on(2 * far - 1, (z + zn - far) % zn, below[far])
            hand_on(2 * far, (z + far) % zn, above[far])
        else:
            hand_on(zn - 1, (z + half) % zn, across)

    for c in maps:
        c.wait()
    for c in asks:
        c.wait_recv()
    hand_on(0, z, mine)
    rim = [fetch(reg.at[:, pl.ds(BLK * b, BLK)], ext.at[b + 1]) for b in range(nbl)]
    prev_c = fetch(prev, prev_v)
    low_c = fetch(low_any, low)
    grad_c = fetch(grad, grad_v)
    couple_c = fetch(couple, couple_v)
    sens_c = fetch(sens, sens_v)
    for far in range(min(2, half), 0, -1):
        arrive(far)
        hand_on_far(far)
    prev_c.wait()
    low_c.wait()
    adj[...] = -jnp.dot(
        low[...], prev_v[...], precision=lax.Precision.HIGHEST, preferred_element_type=F32
    )
    for c in rim:
        c.wait()
    grad_c.wait()
    couple_c.wait()
    for c in near:
        c.wait_recv()

    @pl.when(g == 0)
    def _():
        ext[0] = jnp.zeros((n, BLK), BF16)

    @pl.when(g == rn * dn - 1)
    def _():
        ext[nbl + 1] = jnp.zeros((n, BLK), BF16)

    for k, edge in ((0, 0), (1, rn - 1)):
        for b in range(dbl):
            block = side[k][:, BLK * b : BLK * b + BLK]
            nb[k * dbl + b] = jnp.where(r == edge, jnp.zeros_like(block), block)
    gradient(0, nbl)
    coupling(0, nbl)
    for far in range(3, half + 1):
        arrive(far)
        hand_on_far(far)
    sens_c.wait()
    for c in x_copies:
        c.wait_recv()
    for b in range(nbl):
        lhs = jnp.concatenate([compact[src[b, k]] for k in range(kk)], axis=1)
        part = jnp.dot(lhs, sens_v[b].reshape(kk * BLK, BLK), preferred_element_type=F32)
        adj[:, BLK * b : BLK * b + BLK] += part

    s, gram = gram_local(adj[...])
    s_out[...] = s
    gram = gram * (1.0 / (rn * dn * nbl * BLK))
    lane = lax.broadcasted_iota(jnp.int32, (n // 2, BLK), 1)
    swapped = pltpu.roll(gram, n, 1)
    top, bottom = pl.ds(0, rows // 2), pl.ds(rows // 2, rows // 2)
    gram_hi = jnp.where(lane < n, gram[: n // 2], swapped[n // 2 :])
    gram_lo = jnp.where(lane < n, swapped[: n // 2], gram[n // 2 :])
    for q in range(gn):
        part = slice(rows // 2 * q, rows // 2 * (q + 1))
        gpart[q, top] = gram_hi[part]
        gpart[q, bottom] = gram_lo[part]

    def total(ref, count, target):
        terms = [(ref[q, top], ref[q, bottom]) for q in range(count)]
        while len(terms) > 1:
            paired = []
            for (a, a_low), (b, b_low) in zip(terms[::2], terms[1::2]):
                hi, e = two_sum(a, b)
                paired.append((hi, (a_low + b_low) + e))
            terms = paired + terms[len(paired) * 2 :]
        hi, lo = terms[0]
        big = hi + lo
        target[top] = big
        target[bottom] = lo - (big - hi)

    def exchange(stage, count, mine, box, who, source):
        copies = []
        for o in range(1, count):
            copies.append(
                remote(source(o), box.at[mine], a_send.at[stage, o - 1], a_recv.at[stage, o - 1], who(o))
            )
        return copies

    copies = exchange(0, gn, piece, rs, group, lambda o: gpart.at[(piece + o) % gn])
    rs[piece] = gpart[piece]
    for c in copies:
        c.wait_recv()
    sent += copies
    total(rs, gn, zs.at[z])
    copies = exchange(1, zn, z, zs, along_z, lambda o: zs.at[z])
    for c in copies:
        c.wait_recv()
    sent += copies
    total(zs, zn, ys.at[y])
    copies = exchange(2, yn, y, ys, along_y, lambda o: ys.at[y])
    for c in copies:
        c.wait_recv()
    sent += copies
    total(ys, yn, ag.at[piece])
    copies = exchange(3, gn, piece, ag, group, lambda o: ag.at[piece])
    for c in copies:
        c.wait_recv()
    sent += copies
    hi = jnp.concatenate([ag[q, top] for q in range(gn)], axis=0)
    lo = jnp.concatenate([ag[q, bottom] for q in range(gn)], axis=0)
    g_out[: n // 2, :] = jnp.where(lane < n, hi, pltpu.roll(lo, n, 1))
    g_out[n // 2 :, :] = jnp.where(lane < n, pltpu.roll(hi, n, 1), lo)
    for c in sent + x_copies:
        c.wait_send()


def gather(xn, data, reg, prev, low, sens, src, touched, couple, cmap, grad, gmap):
    zn = lax.axis_size("dev") // xn
    rn = lax.axis_size("region")
    n = data.shape[0]
    nbl, kk = sens.shape[0], sens.shape[1]
    kc, kg = couple.shape[1], grad.shape[1]
    dbl = data.shape[1] // BLK
    gn, yn, dn = 2 * xn, rn // 2, xn * zn
    rows = n // gn
    most = max(gn, zn, yn) - 1
    vm = pl.BlockSpec(memory_space=pltpu.VMEM)
    hbm = pl.BlockSpec(memory_space=pltpu.HBM)
    sem = pltpu.SemaphoreType.DMA
    width = nbl * BLK
    sizes = (xn, zn, rn, nbl, dbl, kk, kc, kg)
    row = touched.reshape(1, dn)
    return pl.pallas_call(
        functools.partial(gather_kernel, sizes),
        out_shape=(
            pltpu.VMEM((SLICES * n, width), BF16),
            pltpu.VMEM((n, BLK), F32),
        ),
        in_specs=[hbm] * 11,
        out_specs=(vm, vm),
        scratch_shapes=[
            tuple(pltpu.VMEM((dbl, n, BLK), BF16) for _ in range(zn)),
            pltpu.VMEM((dn, n, BLK), BF16),
            pltpu.VMEM((max(xn - 1, 1), zn, n, BLK), BF16),
            tuple(pltpu.VMEM((n, dbl * BLK), BF16) for _ in range(2)),
            pltpu.VMEM((2 * dbl, n, BLK), BF16),
            pltpu.VMEM((nbl + 2, n, BLK), BF16),
            pltpu.VMEM((n, width), F32),
            pltpu.VMEM((n, n), F32),
            pltpu.VMEM(sens.shape, BF16),
            pltpu.VMEM(couple.shape, BF16),
            pltpu.VMEM(grad.shape, BF16),
            pltpu.SMEM((1, dn), jnp.int32),
            pltpu.SMEM((nbl, kk), jnp.int32),
            pltpu.SMEM((kc, nbl), jnp.int32),
            pltpu.SMEM((kg, nbl), jnp.int32),
            pltpu.SMEM((max(xn - 1, 1), 1, dn), jnp.int32),
            pltpu.VMEM((n, width), F32),
            pltpu.VMEM((gn, rows, BLK), F32),
            pltpu.VMEM((gn, rows, BLK), F32),
            pltpu.VMEM((zn, rows, BLK), F32),
            pltpu.VMEM((yn, rows, BLK), F32),
            pltpu.VMEM((gn, rows, BLK), F32),
            sem((dbl + nbl + 10,)),
            sem((2, zn // 2, dbl)),
            sem((2, zn // 2, dbl)),
            sem((xn, zn)),
            sem((xn, zn)),
            sem((4,)),
            sem((4,)),
            sem((xn,)),
            sem((xn,)),
            sem((4, most)),
            sem((4, most)),
        ],
        compiler_params=pltpu.CompilerParams(
            collective_id=0, has_side_effects=True, vmem_limit_bytes=60 * 2**20
        ),
        name="gather",
    )(data, reg, prev, low, row, sens, src, couple, cmap.T, grad, gmap.T)


def local(
    data_panel, reg_panel, prev_panel, lower_block, sens_tiles, sens_src, touched,
    couple_tiles, couple_map, grad_tiles, grad_map,
):
    s, g = gather(
        X_CHIPS, data_panel, reg_panel, prev_panel, lower_block, sens_tiles, sens_src, touched,
        couple_tiles, couple_map, grad_tiles, grad_map,
    )
    return finish(g, s)


def solution(mesh):
    return jax.shard_map(
        local,
        mesh=mesh,
        in_specs=(
            P(None, ("region", "dev")),
            P(None, ("region", "dev")),
            P(None, ("region", "dev")),
            P(),
            P(("region", "dev"), None, None, None),
            P(("region", "dev"), None),
            P(("region", "dev")),
            P(("region", "dev"), None, None, None),
            P(("region", "dev"), None),
            P(("region", "dev"), None, None, None),
            P(("region", "dev"), None),
        ),
        out_specs=(P(None, ("region", "dev")), P()),
        check_vma=False,
    )
```

```python
import functools

import jax
import jax.numpy as jnp
from jax import lax
from jax.experimental import pallas as pl
from jax.experimental.pallas import tpu as pltpu
from jax.sharding import PartitionSpec as P

F32 = jnp.float32
BF16 = jnp.bfloat16
SLICES = 4
BLK = 128
X_CHIPS = 4


def two_sum(a, b):
    s = a + b
    t = s - a
    return s, (a - (s - t)) + (b - t)


def cut(value, sigma):
    top = (value + sigma) - sigma
    return top, value - top


def eliminate(aug, rows):
    blocks = [aug[8 * b : 8 * b + 8, :] for b in range(rows // 8)]
    sub = lax.broadcasted_iota(jnp.int32, (8, 128), 0)
    out = []
    for b in range(rows // 8):
        live = len(blocks)
        cols = [
            [jnp.broadcast_to(blk[:, 8 * b + k : 8 * b + k + 1], (8, 128)) for blk in blocks]
            for k in range(8)
        ]
        head = blocks[0]
        pivots = jnp.ones((8, 128), F32)
        for k in range(8):
            pivot = jnp.broadcast_to(cols[k][0][k : k + 1, :], (8, 128))
            inv = 1.0 / pivot
            pivots = jnp.where(sub == k, pivot, pivots)
            factor = [c * inv for c in cols[k]]
            factor[0] = jnp.where(sub > k, factor[0], 0.0)
            for m in range(k + 1, 8):
                across = jnp.broadcast_to(cols[m][0][k : k + 1, :], (8, 128))
                cols[m] = [c - f * across for c, f in zip(cols[m], factor)]
            row = jnp.broadcast_to(head[k : k + 1, :], (8, 128))
            head = head - factor[0] * row
            blocks = [head] + [blk - f * row for blk, f in zip(blocks[1:], factor[1:])]
        root = lax.rsqrt(pivots)
        root = root * (1.5 - (0.5 * pivots) * (root * root))
        out.append(head * root)
        blocks = blocks[1:]
    return jnp.concatenate(out, axis=0)


def split3(v):
    hi = v.astype(BF16)
    r = v - hi.astype(F32)
    mid = r.astype(BF16)
    return hi, mid, (r - mid.astype(F32)).astype(BF16)


def finish_kernel(g_ref, s_ref, q_ref, f_ref):
    n = 64
    g = g_ref[...]
    lane = lax.broadcasted_iota(jnp.int32, (n, 128), 1)
    subl = lax.broadcasted_iota(jnp.int32, (n, 128), 0)
    left = lane < n
    eye_right = (lane == subl + n).astype(F32)
    eye = (lane == subl).astype(F32)
    low_part = jnp.where(left, pltpu.roll(g, n, 1), 0.0)
    hi_part = jnp.where(left, g, 0.0)
    first = eliminate(hi_part + eye_right, n)

    w = jnp.where(left, pltpu.roll(first, n, 1), 0.0)
    wsig = jnp.max(jnp.abs(w), axis=1, keepdims=True) * 131072.0
    gsig = jnp.max(jnp.abs(hi_part), axis=0, keepdims=True) * 131072.0
    ws = []
    r = w
    for i in range(4):
        top, r = cut(r, wsig * (2.0 ** (-7 * i)))
        ws.append(top.astype(BF16)[:, :n])
    gs = []
    r = hi_part
    for i in range(3):
        top, r = cut(r, gsig * (2.0 ** (-7 * i)))
        gs.append(top.astype(BF16))
    r = r + low_part
    for i in range(3, 6):
        top, r = cut(r, gsig * (2.0 ** (-7 * i)))
        gs.append(top.astype(BF16))
    hi = lo = None
    for level in range(6):
        pairs = [(i, level - i) for i in range(4) if 0 <= level - i < 6]
        lhs = jnp.concatenate([ws[i] for i, _ in pairs], axis=1)
        rhs = jnp.concatenate([gs[j] for _, j in pairs], axis=0)
        term = jnp.dot(lhs, rhs, preferred_element_type=F32)
        if hi is None:
            hi, lo = term, jnp.zeros_like(term)
        else:
            hi, e = two_sum(hi, term)
            lo = lo + e
    t = hi + lo
    g2 = lax.dot_general(
        t, w, (((1,), (1,)), ((), ())), precision=lax.Precision.HIGHEST, preferred_element_type=F32
    )
    zero = jnp.zeros((n, n), F32)
    second = eliminate(jnp.concatenate([g2, zero], axis=1) + eye_right, n)
    w2 = jnp.where(left, pltpu.roll(second, n, 1), 0.0)
    both = jnp.dot(second[:, :n], first[:, :n], precision=lax.Precision.HIGHEST, preferred_element_type=F32)
    f_ref[...] = both
    m = jnp.dot(w2[:, :n], w[:, :n], precision=lax.Precision.HIGHEST, preferred_element_type=F32)
    parts = jnp.concatenate([jnp.concatenate([p] * SLICES, axis=1) for p in split3(m)], axis=0)
    for c in range(4):
        res = jnp.dot(parts, s_ref[:, 256 * c : 256 * c + 256], preferred_element_type=F32)
        q_ref[:, 256 * c : 256 * c + 256] = res[:n] + (res[n : 2 * n] + res[2 * n :])


def finish(g, s):
    vm = pl.BlockSpec(memory_space=pltpu.VMEM)
    return pl.pallas_call(
        finish_kernel,
        out_shape=(jax.ShapeDtypeStruct((64, 1024), F32), jax.ShapeDtypeStruct((64, 64), F32)),
        in_specs=[vm, vm],
        out_specs=(vm, vm),
        compiler_params=pltpu.CompilerParams(vmem_limit_bytes=32 * 2**20),
        name="finish",
    )(g, s)


def gram_local(a):
    n = 64
    sig = jnp.max(jnp.abs(a), axis=1, keepdims=True) * 131072.0
    parts = []
    r = a
    for i in range(SLICES):
        top, r = cut(r, sig * (2.0 ** (-7 * i)))
        parts.append(top.astype(BF16))
    s = jnp.concatenate(parts, axis=0)
    p = lax.dot_general(s, s, (((1,), (1,)), ((), ())), preferred_element_type=F32)
    order = [(0, 0), (1, 0), (0, 1), (2, 0), (1, 1), (3, 0), (2, 1), (3, 1)]
    hi = lo = None
    for i, h in order:
        term = p[n * i : n * i + n, 128 * h : 128 * h + 128]
        if hi is None:
            hi, lo = term, jnp.zeros_like(term)
        else:
            hi, e = two_sum(hi, term)
            lo = lo + e
    hi, e = two_sum(hi, pltpu.roll(hi, n, 1))
    lo = (lo + pltpu.roll(lo, n, 1)) + e
    hi, lo = hi + lo, lo - ((hi + lo) - hi)
    lane = lax.broadcasted_iota(jnp.int32, (n, 128), 1)
    return s, jnp.where(lane < n, hi, pltpu.roll(lo, n, 1))


MESH = pl.DeviceIdType.MESH


def gather_kernel(
    sizes,
    data, reg, prev, low_any, touched_any, sens, src_any, couple, cmap_any, grad, gmap_any,
    s_out, g_out,
    zbs, compact, xs, side, nb, ext, prev_v, low, sens_v, couple_v, grad_v, touched, src, cmap, gmap, asked, adj, gpart, rs, zs, ys, ag,
    l_sem, z_send, z_recv, x_send, x_recv, n_send, n_recv, t_send, t_recv, a_send, a_recv,
):
    xn, zn, rn, nbl, dbl, kk, kc, kg = sizes
    n = 64
    yn, gn = rn // 2, 2 * xn
    dn = xn * zn
    rows = n // gn
    half = zn // 2
    r = lax.axis_index("region")
    d = lax.axis_index("dev")
    y, core = r // 2, r % 2
    z, x = d // xn, d % xn
    piece = x * 2 + core

    mine = zbs[0]
    below = [mine] + list(zbs[1:half])
    above = [mine] + list(zbs[half : 2 * half - 1])
    across = zbs[2 * half - 1]

    local = []

    def fetch(source, target):
        c = pltpu.make_async_copy(source, target, l_sem.at[len(local)])
        c.start()
        local.append(c)
        return c

    own = [fetch(data.at[:, pl.ds(BLK * b, BLK)], mine.at[b]) for b in range(dbl)]
    maps = [fetch(a, b) for a, b in ((touched_any, touched), (src_any, src), (cmap_any, cmap), (gmap_any, gmap))]
    def group(o):
        q = (piece + o) % gn
        return (y * 2 + q % 2, z * xn + q // 2)

    def along_z(o):
        return (r, ((z + o) % zn) * xn + x)

    def along_y(o):
        return (((y + o) % yn) * 2 + core, d)

    def along_x(o):
        return (r, z * xn + (x + o) % xn)

    up, down = ((r + 1) % rn, d), ((r + rn - 1) % rn, d)
    g = r * dn + d
    g_up, g_down = (g + 1) % (rn * dn), (g + rn * dn - 1) % (rn * dn)
    after, before = (g_up // dn, g_up % dn), (g_down // dn, g_down % dn)
    reached = [group(o) for o in range(1, gn)] + [along_z(o) for o in range(1, zn) if min(o, zn - o) <= 2]
    reached += [along_y(o) for o in range(1, yn)] + [up, down, after, before]
    barrier = pltpu.get_barrier_semaphore()
    for who in reached:
        pl.semaphore_signal(barrier, inc=1, device_id=who, device_id_type=MESH)
    pl.semaphore_wait(barrier, len(reached))

    def remote(source, target, send, recv, who):
        c = pltpu.make_async_remote_copy(
            src_ref=source, dst_ref=target, send_sem=send, recv_sem=recv,
            device_id=who, device_id_type=MESH,
        )
        c.start()
        return c

    sent = []
    asks = []
    for o in range(1, xn):
        asks.append(remote(touched_any, asked.at[xn - o - 1], t_send.at[o - 1], t_recv.at[o - 1], along_x(o)))
    sent += asks
    def pass_on(way, far, b):
        held = (below, above)[way]
        target = held[far] if far < half else across
        hops = far if far <= 2 else far - 2
        source = (mine if far <= 2 else held[2]).at[b]
        c = remote(source, target.at[b], z_send.at[way, far - 1, b], z_recv.at[way, far - 1, b],
                   along_z(hops if way == 0 else zn - hops))
        sent.append(c)
        moves[way, far, b] = c

    def parts(far):
        return [(way, b) for b in range(dbl) for way in range(2) if far < half or b // (dbl // 2) == way]

    moves = {}
    x_copies = []

    def hand_on(slot, zz, held):
        for o in sorted(range(1, xn), key=lambda o: -min(o, xn - o)):
            xs[o - 1, slot] = held[asked[o - 1, 0, zz * xn + x]]
            x_copies.append(
                remote(xs.at[o - 1, slot], compact.at[zz * xn + x],
                       x_send.at[o - 1, slot], x_recv.at[o - 1, slot], along_x(o))
            )
        compact[zz * xn + x] = held[touched[0, zz * xn + x]]

    for c in own:
        c.wait()
    for far in range(min(2, half), 0, -1):
        for way, b in parts(far):
            pass_on(way, far, b)
    near = [
        remote(data, side[0], n_send.at[0], n_recv.at[0], up),
        remote(data, side[1], n_send.at[1], n_recv.at[1], down),
        remote(reg.at[:, pl.ds(BLK * (nbl - 1), BLK)], ext.at[0], n_send.at[2], n_recv.at[2], after),
        remote(reg.at[:, pl.ds(0, BLK)], ext.at[nbl + 1], n_send.at[3], n_recv.at[3], before),
    ]
    sent += near

    def gradient(first, last):
        for b in range(first, last):
            lhs = jnp.concatenate([ext[gmap[j, b]] for j in range(kg)], axis=1)
            part = jnp.dot(lhs, grad_v[b].reshape(kg * BLK, BLK), preferred_element_type=F32)
            adj[:, BLK * b : BLK * b + BLK] += 0.5 * part

    def coupling(first, last):
        for b in range(first, last):
            lhs = jnp.concatenate([nb[cmap[j, b]] for j in range(kc)], axis=1)
            part = jnp.dot(lhs, couple_v[b].reshape(kc * BLK, BLK), preferred_element_type=F32)
            adj[:, BLK * b : BLK * b + BLK] += part

    def arrive(far):
        for way, b in parts(far):
            moves[way, far, b].wait_recv()
            if far == 2:
                for further in range(half, 2, -1):
                    if (way, b) in parts(further):
                        pass_on(way, further, b)

    def hand_on_far(far):
        if far < half:
            hand_on(2 * far - 1, (z + zn - far) % zn, below[far])
            hand_on(2 * far, (z + far) % zn, above[far])
        else:
            hand_on(zn - 1, (z + half) % zn, across)

    for c in maps:
        c.wait()
    for c in asks:
        c.wait_recv()
    hand_on(0, z, mine)
    rim = [fetch(reg.at[:, pl.ds(BLK * b, BLK)], ext.at[b + 1]) for b in range(nbl)]
    prev_c = fetch(prev, prev_v)
    low_c = fetch(low_any, low)
    grad_c = fetch(grad, grad_v)
    couple_c = fetch(couple, couple_v)
    sens_c = fetch(sens, sens_v)
    for far in range(min(2, half), 0, -1):
        arrive(far)
        hand_on_far(far)
    prev_c.wait()
    low_c.wait()
    adj[...] = -jnp.dot(
        low[...], prev_v[...], precision=lax.Precision.HIGHEST, preferred_element_type=F32
    )
    for c in rim:
        c.wait()
    grad_c.wait()
    couple_c.wait()
    for c in near:
        c.wait_recv()

    @pl.when(g == 0)
    def _():
        ext[0] = jnp.zeros((n, BLK), BF16)

    @pl.when(g == rn * dn - 1)
    def _():
        ext[nbl + 1] = jnp.zeros((n, BLK), BF16)

    for k, edge in ((0, 0), (1, rn - 1)):
        for b in range(dbl):
            block = side[k][:, BLK * b : BLK * b + BLK]
            nb[k * dbl + b] = jnp.where(r == edge, jnp.zeros_like(block), block)
    gradient(0, nbl)
    coupling(0, nbl)
    for far in range(3, half + 1):
        arrive(far)
        hand_on_far(far)
    sens_c.wait()
    for c in x_copies:
        c.wait_recv()
    for b in range(nbl):
        lhs = jnp.concatenate([compact[src[b, k]] for k in range(kk)], axis=1)
        part = jnp.dot(lhs, sens_v[b].reshape(kk * BLK, BLK), preferred_element_type=F32)
        adj[:, BLK * b : BLK * b + BLK] += part

    s, gram = gram_local(adj[...])
    s_out[...] = s
    gram = gram * (1.0 / (rn * dn * nbl * BLK))
    lane = lax.broadcasted_iota(jnp.int32, (n // 2, BLK), 1)
    swapped = pltpu.roll(gram, n, 1)
    top, bottom = pl.ds(0, rows // 2), pl.ds(rows // 2, rows // 2)
    gram_hi = jnp.where(lane < n, gram[: n // 2], swapped[n // 2 :])
    gram_lo = jnp.where(lane < n, swapped[: n // 2], gram[n // 2 :])
    for q in range(gn):
        part = slice(rows // 2 * q, rows // 2 * (q + 1))
        gpart[q, top] = gram_hi[part]
        gpart[q, bottom] = gram_lo[part]

    def total(ref, count, target):
        terms = [(ref[q, top], ref[q, bottom]) for q in range(count)]
        while len(terms) > 1:
            paired = []
            for (a, a_low), (b, b_low) in zip(terms[::2], terms[1::2]):
                hi, e = two_sum(a, b)
                paired.append((hi, (a_low + b_low) + e))
            terms = paired + terms[len(paired) * 2 :]
        hi, lo = terms[0]
        big = hi + lo
        target[top] = big
        target[bottom] = lo - (big - hi)

    def exchange(stage, count, mine, box, who, source):
        copies = []
        for o in sorted(range(1, count), key=lambda o: -min(o, count - o)):
            copies.append(
                remote(source(o), box.at[mine], a_send.at[stage, o - 1], a_recv.at[stage, o - 1], who(o))
            )
        return copies

    copies = exchange(0, gn, piece, rs, group, lambda o: gpart.at[(piece + o) % gn])
    rs[piece] = gpart[piece]
    for c in sent + x_copies:
        c.wait_send()
    last = copies
    for c in copies:
        c.wait_recv()
    total(rs, gn, zs.at[z])
    copies = exchange(1, zn, z, zs, along_z, lambda o: zs.at[z])
    for c in last:
        c.wait_send()
    last = copies
    for c in copies:
        c.wait_recv()
    total(zs, zn, ys.at[y])
    copies = exchange(2, yn, y, ys, along_y, lambda o: ys.at[y])
    for c in last:
        c.wait_send()
    last = copies
    for c in copies:
        c.wait_recv()
    total(ys, yn, ag.at[piece])
    copies = exchange(3, gn, piece, ag, group, lambda o: ag.at[piece])
    for c in last:
        c.wait_send()
    last = copies
    for c in copies:
        c.wait_recv()
    hi = jnp.concatenate([ag[q, top] for q in range(gn)], axis=0)
    lo = jnp.concatenate([ag[q, bottom] for q in range(gn)], axis=0)
    g_out[: n // 2, :] = jnp.where(lane < n, hi, pltpu.roll(lo, n, 1))
    g_out[n // 2 :, :] = jnp.where(lane < n, pltpu.roll(hi, n, 1), lo)
    for c in last:
        c.wait_send()


def gather(xn, data, reg, prev, low, sens, src, touched, couple, cmap, grad, gmap):
    zn = lax.axis_size("dev") // xn
    rn = lax.axis_size("region")
    n = data.shape[0]
    nbl, kk = sens.shape[0], sens.shape[1]
    kc, kg = couple.shape[1], grad.shape[1]
    dbl = data.shape[1] // BLK
    gn, yn, dn = 2 * xn, rn // 2, xn * zn
    rows = n // gn
    most = max(gn, zn, yn) - 1
    vm = pl.BlockSpec(memory_space=pltpu.VMEM)
    hbm = pl.BlockSpec(memory_space=pltpu.HBM)
    sem = pltpu.SemaphoreType.DMA
    width = nbl * BLK
    sizes = (xn, zn, rn, nbl, dbl, kk, kc, kg)
    row = touched.reshape(1, dn)
    return pl.pallas_call(
        functools.partial(gather_kernel, sizes),
        out_shape=(
            pltpu.VMEM((SLICES * n, width), BF16),
            pltpu.VMEM((n, BLK), F32),
        ),
        in_specs=[hbm] * 11,
        out_specs=(vm, vm),
        scratch_shapes=[
            tuple(pltpu.VMEM((dbl, n, BLK), BF16) for _ in range(zn)),
            pltpu.VMEM((dn, n, BLK), BF16),
            pltpu.VMEM((max(xn - 1, 1), zn, n, BLK), BF16),
            tuple(pltpu.VMEM((n, dbl * BLK), BF16) for _ in range(2)),
            pltpu.VMEM((2 * dbl, n, BLK), BF16),
            pltpu.VMEM((nbl + 2, n, BLK), BF16),
            pltpu.VMEM((n, width), F32),
            pltpu.VMEM((n, n), F32),
            pltpu.VMEM(sens.shape, BF16),
            pltpu.VMEM(couple.shape, BF16),
            pltpu.VMEM(grad.shape, BF16),
            pltpu.SMEM((1, dn), jnp.int32),
            pltpu.SMEM((nbl, kk), jnp.int32),
            pltpu.SMEM((kc, nbl), jnp.int32),
            pltpu.SMEM((kg, nbl), jnp.int32),
            pltpu.SMEM((max(xn - 1, 1), 1, dn), jnp.int32),
            pltpu.VMEM((n, width), F32),
            pltpu.VMEM((gn, rows, BLK), F32),
            pltpu.VMEM((gn, rows, BLK), F32),
            pltpu.VMEM((zn, rows, BLK), F32),
            pltpu.VMEM((yn, rows, BLK), F32),
            pltpu.VMEM((gn, rows, BLK), F32),
            sem((dbl + nbl + 10,)),
            sem((2, zn // 2, dbl)),
            sem((2, zn // 2, dbl)),
            sem((xn, zn)),
            sem((xn, zn)),
            sem((4,)),
            sem((4,)),
            sem((xn,)),
            sem((xn,)),
            sem((4, most)),
            sem((4, most)),
        ],
        compiler_params=pltpu.CompilerParams(
            collective_id=0, has_side_effects=True, vmem_limit_bytes=60 * 2**20
        ),
        name="gather",
    )(data, reg, prev, low, row, sens, src, couple, cmap.T, grad, gmap.T)


def local(
    data_panel, reg_panel, prev_panel, lower_block, sens_tiles, sens_src, touched,
    couple_tiles, couple_map, grad_tiles, grad_map,
):
    s, g = gather(
        X_CHIPS, data_panel, reg_panel, prev_panel, lower_block, sens_tiles, sens_src, touched,
        couple_tiles, couple_map, grad_tiles, grad_map,
    )
    return finish(g, s)


def solution(mesh):
    return jax.shard_map(
        local,
        mesh=mesh,
        in_specs=(
            P(None, ("region", "dev")),
            P(None, ("region", "dev")),
            P(None, ("region", "dev")),
            P(),
            P(("region", "dev"), None, None, None),
            P(("region", "dev"), None),
            P(("region", "dev")),
            P(("region", "dev"), None, None, None),
            P(("region", "dev"), None),
            P(("region", "dev"), None, None, None),
            P(("region", "dev"), None),
        ),
        out_specs=(P(None, ("region", "dev")), P()),
        check_vma=False,
    )
```
